256 devices in a mesh: band: 16 (over z_lo, y), plane: 16 (over x, z_hi, core).
Axes of the slice: x: 4, y: 4, z: 8 (z_hi: 2, z_lo: 4; z = z_hi * 4 + z_lo), core: 2. Of those that a mesh axis runs over, the one named last changes fastest.
Arguments:
- coeffs: float32 [16, 4, 65, 2048], P('band', None, None, 'plane'), may hold values from -6 to 6
- potential: float32 [128, 128, 128], P('plane', 'band'), may hold values from -6 to 6
- stick_map: int32 [3, 2048], replicated, may hold values from -32 to 32, as said below
Outputs:
- applied_coeffs: float32 [16, 4, 65, 2048], P('band', None, None, 'plane')
The draws below stay inside these ranges and needn't reach their ends.
Inputs may be any that keep to these rules, and one draw needn't show every extreme that they name: `stick_map`: column s describes stick slot s: rows 0 and 1 are its G_x and G_y, row 2 its half-height h, or -1 for an empty slot (then G_x = G_y = 0). The live slots hold every column (x, y) with x*x + y*y <= 32 squared and x > 0, or x = 0 and y > 0, exactly once, with h the largest integer for which x*x + y*y + h*h <= 32 squared. Which slot holds which column is drawn.
All inputs are finite; a program needn't handle non-finite values.
Results may differ from the reference program's by a relative error of at most 0.00007.
Values sent between devices are 32-bit elements; how exact they have to be, the bound alone decides.
A program may use at most 64 MiB of HBM per device.

```python
import jax
import jax.numpy as jnp
from jax import lax

GRID = 128
RADIUS = 32
STICKS = 2048
ZSPAN = 65
PAIRS = 16


def draw_stick_map(key, part):
    side_len = 2 * RADIUS + 1
    lattice = jnp.arange(side_len * side_len, dtype=jnp.int32)
    candidate_x = lattice // side_len - RADIUS
    candidate_y = lattice % side_len - RADIUS
    distance = candidate_x * candidate_x + candidate_y * candidate_y
    inside = (distance <= RADIUS * RADIUS) & ((candidate_x > 0) | (candidate_x == 0) & (candidate_y > 0))
    levels = jnp.arange(1, RADIUS + 1, dtype=jnp.int32)
    heights = jnp.sum((levels[None, :] * levels[None, :] <= RADIUS * RADIUS - distance[:, None]).astype(jnp.int32), axis=1)
    ranking = jnp.argsort(jnp.where(inside, 0, 1).astype(jnp.int32), stable=True)
    chosen = ranking[:STICKS]
    is_live = inside[chosen]
    column_x = jnp.where(is_live, candidate_x[chosen], 0)
    column_y = jnp.where(is_live, candidate_y[chosen], 0)
    column_h = jnp.where(is_live, heights[chosen], -1)
    shuffle = jax.random.permutation(jax.random.fold_in(key, 7), STICKS)
    return jnp.stack([column_x[shuffle], column_y[shuffle], column_h[shuffle]]).astype(jnp.int32)


def block_scale(rng, dims, shards, least, high):
    level, own = 1.0, jax.random.fold_in(rng, 6)
    for axis_at, shards_of in shards:
        draws = jnp.exp(jax.random.uniform(jax.random.fold_in(own, axis_at), (shards_of,), jnp.float32, least / len(shards), high / len(shards)))
        level = level * jnp.repeat(draws, dims[axis_at] // shards_of).reshape([-1 if axis == axis_at else 1 for axis in range(len(dims))])
    return level


def gaussian(own_key, extent, spread, bound, pieces=(), held_as=jnp.bfloat16):
    result = jax.random.normal(own_key, extent, jnp.float32) * spread
    if len(pieces) > 0:
        result = block_scale(own_key, extent, pieces, -0.22, 0.18) * result
    return jnp.clip(result, min=-bound, max=bound).astype(held_as)


def setup_inputs(seed: int = 0) -> dict:
    arg_keys = jax.random.split(jax.random.key(seed), 4)
    coeffs = gaussian(arg_keys[0], (PAIRS, 4, ZSPAN, STICKS), 1.0, 6.0, ((0, 16), (3, 16)), jnp.float32)
    potential = gaussian(arg_keys[1], (GRID, GRID, GRID), 1.0, 6.0, ((0, 16), (1, 16)), jnp.float32)
    stick_map = draw_stick_map(jax.random.fold_in(arg_keys[3], 71), 0)
    return {"coeffs": coeffs, "potential": potential, "stick_map": stick_map}


def reference(coeffs, potential, stick_map):
    stick_x = stick_map[0]
    stick_y = stick_map[1]
    heights = stick_map[2]
    depth_ids = jnp.arange(ZSPAN, dtype=jnp.int32) - RADIUS
    live_mask = jnp.abs(depth_ids)[:, None] <= heights[None, :]
    shape_two = (ZSPAN, STICKS)
    plus_x = jnp.broadcast_to(jnp.mod(stick_x, GRID)[None, :], shape_two).astype(jnp.int32)
    plus_y = jnp.broadcast_to(jnp.mod(stick_y, GRID)[None, :], shape_two).astype(jnp.int32)
    plus_z = jnp.broadcast_to(jnp.mod(depth_ids, GRID)[:, None], shape_two).astype(jnp.int32)
    minus_x = jnp.broadcast_to(jnp.mod(-stick_x, GRID)[None, :], shape_two).astype(jnp.int32)
    minus_y = jnp.broadcast_to(jnp.mod(-stick_y, GRID)[None, :], shape_two).astype(jnp.int32)
    minus_z = jnp.broadcast_to(jnp.mod(-depth_ids, GRID)[:, None], shape_two).astype(jnp.int32)
    field = jnp.transpose(potential, (1, 2, 0))
    volume = float(GRID) ** 3

    def one_pair(coeff_block):
        masked = jnp.where(live_mask[None], coeff_block, jnp.zeros_like(coeff_block))
        first_orb = lax.complex(masked[0], masked[1])
        second_orb = lax.complex(masked[2], masked[3])
        packed = first_orb + 1j * second_orb
        mirrored = jnp.conj(first_orb) + 1j * jnp.conj(second_orb)
        spectrum = jnp.zeros((GRID, GRID, GRID), packed.dtype)
        spectrum = spectrum.at[plus_x, plus_y, plus_z].add(packed)
        spectrum = spectrum.at[minus_x, minus_y, minus_z].add(mirrored)
        orbitals = jnp.fft.ifftn(spectrum) * volume
        applied = jnp.fft.fftn(orbitals * field) / volume
        direct = applied[plus_x, plus_y, plus_z]
        opposite = jnp.conj(applied[minus_x, minus_y, minus_z])
        new_first = 0.5 * (direct + opposite)
        new_second = -0.5j * (direct - opposite)
        stacked = jnp.stack([jnp.real(new_first), jnp.imag(new_first), jnp.real(new_second), jnp.imag(new_second)])
        stacked = stacked.astype(coeff_block.dtype)
        return jnp.where(live_mask[None], stacked, jnp.zeros_like(stacked))

    return lax.map(one_pair, coeffs)
```

```python
import functools

import jax
import jax.numpy as jnp
import ml_dtypes
import numpy as np
from jax import lax
from jax.experimental import pallas as pl
from jax.experimental.pallas import tpu as pltpu
from jax.sharding import PartitionSpec as P

MESH = pl.DeviceIdType.MESH
GRID = 128
RADIUS = 32
BF = jnp.bfloat16
F32 = jnp.float32


def _halves(table):
    high = table.astype(ml_dtypes.bfloat16)
    low = (table - high.astype(np.float64)).astype(ml_dtypes.bfloat16)
    return high, low


def _left(table):
    high, low = _halves(table)
    return np.concatenate([high, low, high], axis=1)


def _right(table):
    high, low = _halves(table)
    return np.concatenate([high, low, high], axis=0)


def _trig(left, right):
    turns = np.mod(np.outer(left, right), GRID) * (2.0 * np.pi / GRID)
    return np.cos(turns), np.sin(turns)


def tables():
    points = np.arange(GRID)
    depth = np.arange(2 * RADIUS + 1) - RADIUS
    span = depth.size
    cos, sin = _trig(points, depth)
    zf = np.zeros((16, 2, 8, 2, 80))
    cos, sin = cos.reshape(16, 8, span), sin.reshape(16, 8, span)
    zf[:, 0, :, 0, :span], zf[:, 0, :, 1, :span] = cos, -sin
    zf[:, 1, :, 0, :span], zf[:, 1, :, 1, :span] = sin, cos
    zf = _left(zf.reshape(256, 160))
    zb = np.zeros((2, 72, 16, 2, 8))
    cos, sin = np.moveaxis(cos, 2, 0), np.moveaxis(sin, 2, 0)
    zb[0, :span, :, 0], zb[0, :span, :, 1] = cos, sin
    zb[1, :span, :, 0], zb[1, :span, :, 1] = -sin, cos
    zb = _left(zb.reshape(144, 256))
    cos, sin = _trig(np.arange(64) - 31, points)
    wy = np.zeros((2, 2, 64, 2, GRID))
    wb = np.zeros((2, 2, GRID, 2, 2, 64))
    for i in range(2):
        wy[i, i, :, 0], wy[i, i, :, 1] = cos, sin
        wb[i, 0, :, 0, i], wb[i, 1, :, 0, i] = cos.T, sin.T
        wb[i, 0, :, 1, i], wb[i, 1, :, 1, i] = -sin.T, cos.T
    wy = np.stack([_right(wy[i].reshape(128, 256)) for i in range(2)])
    wb = _right(wb.reshape(512, 256))
    cos, sin = _trig(np.arange(32), points)
    base = np.zeros((5, 2, 8, GRID))
    base[:4, 0], base[:4, 1] = cos.reshape(4, 8, GRID), -sin.reshape(4, 8, GRID)
    cos, sin = _trig(np.array([RADIUS]), points)
    base[4, 0, 0], base[4, 1, 0] = cos[0] - 1.0, -sin[0]
    base = base.reshape(80, GRID)
    xf, xb = _left(base.T), _left(base)
    return zf, wy, xf, xb, wb, zb


def halves(value):
    high = value.astype(BF)
    return high, (value - high.astype(F32)).astype(BF)


def mm(left, right):
    return jnp.dot(left, right, preferred_element_type=F32)


def kernel(
    n_z, n_y,
    c_ref, p_ref, sm_ref, zf_h, wy_h, xf_h, xb_h, wb_h, zb_h,
    o_ref,
    zf, wy, xf, xb, wb, zb,
    xs, zs, r1, s2, r2, slab, lt, dm, m1, gs, bs, cs, sp, og,
    c_sem, a_s, a_r, b_s, b_r, gz_s, gz_r, gy_s, gy_r, own_sem,
):
    band = lax.axis_index("band")
    me = lax.axis_index("plane")
    z_me, y_me = band // n_y, lax.rem(band, n_y)
    span = c_ref.shape[2]

    loads = [
        pltpu.make_async_copy(src, dst, c_sem.at[n])
        for n, (src, dst) in enumerate(
            [(zf_h, zf), (wy_h, wy), (xf_h, xf), (xb_h, xb), (wb_h, wb), (zb_h, zb)]
        )
    ]
    for load in loads:
        load.start()

    def z_peer(k):
        return lax.rem(z_me + k, n_z) * n_y + y_me

    def y_peer(k):
        return z_me * n_y + lax.rem(y_me + k, n_y)

    barrier = pltpu.get_barrier_semaphore()
    for k in range(1, 16):
        pl.semaphore_signal(
            barrier, inc=1, device_id={"plane": lax.rem(me + k, 16)}, device_id_type=MESH
        )
    for k in range(1, n_z):
        pl.semaphore_signal(barrier, inc=1, device_id={"band": z_peer(k)}, device_id_type=MESH)
    for k in range(1, n_y):
        pl.semaphore_signal(barrier, inc=1, device_id={"band": y_peer(k)}, device_id_type=MESH)

    heights = sm_ref[2:3, pl.ds(pl.multiple_of(me * 128, 128), 128)]
    live = jnp.abs(lax.broadcasted_iota(jnp.int32, (span, 128), 0) - RADIUS) <= heights
    xs[:, 64:80, :] = jnp.zeros((2, 16, 256), F32)
    for orb in range(2):
        for c in range(2):
            xs[c, 0:span, orb * 128 : orb * 128 + 128] = jnp.where(
                live, c_ref[0, 2 * orb + c], 0.0
            )
    high, low = halves(xs[...].reshape(160, 256))
    loads[0].wait()
    zs[...] = mm(zf[...], jnp.concatenate([high, high, low], axis=0)).reshape(16, 16, 256)

    pl.semaphore_wait(barrier, 15 + n_z - 1 + n_y - 1)

    def a_copy(k):
        to = lax.rem(me + k, 16)
        return pltpu.make_async_remote_copy(
            src_ref=zs.at[to], dst_ref=r1.at[me],
            send_sem=a_s.at[k], recv_sem=a_r.at[k],
            device_id={"plane": to}, device_id_type=MESH,
        )

    def b_copy(k):
        to = lax.rem(me + k, 16)
        return pltpu.make_async_remote_copy(
            src_ref=s2.at[to], dst_ref=r2.at[me],
            send_sem=b_s.at[k], recv_sem=b_r.at[k],
            device_id={"plane": to}, device_id_type=MESH,
        )

    def gz_copy(k):
        return pltpu.make_async_remote_copy(
            src_ref=p_ref, dst_ref=slab.at[y_me, z_me],
            send_sem=gz_s.at[k], recv_sem=gz_r.at[k],
            device_id={"band": z_peer(k)}, device_id_type=MESH,
        )

    def gy_copy(k):
        return pltpu.make_async_remote_copy(
            src_ref=slab.at[y_me], dst_ref=slab.at[y_me],
            send_sem=gy_s.at[k], recv_sem=gy_r.at[k],
            device_id={"band": y_peer(k)}, device_id_type=MESH,
        )

    for k in range(1, n_z):
        gz_copy(k).start()
    for k in range(1, 16):
        a_copy(k).start()
    own = pltpu.make_async_copy(p_ref, slab.at[y_me, z_me], own_sem)
    own.start()
    r1[me] = zs[me]

    stick_x, stick_y = sm_ref[0:1, :], sm_ref[1:2, :]
    d_of = stick_x & 7
    lane_of = ((stick_x >> 3) & 3) * 64 + stick_y + 31
    for n in range(16):
        rows = lax.broadcasted_iota(jnp.int32, (16, 2048), 0) + n * 16
        lt[n * 16 : n * 16 + 16, :] = jnp.where(rows == lane_of, 1.0, 0.0).astype(BF)
    d_rows = jnp.broadcast_to(d_of, (16, 2048))
    for d in range(8):
        dm[d] = jnp.where(d_rows == d, 1.0, 0.0).astype(BF)

    own.wait()
    for k in range(1, n_z):
        gz_copy(k).wait_recv()
    for k in range(1, n_y):
        gy_copy(k).start()

    for k in range(1, 16):
        a_copy(k).wait_recv()

    for r in range(16):
        lanes = slice(r * 128, r * 128 + 128)
        for h, part in enumerate(halves(r1[r])):
            for orb in range(2):
                piece = part[:, orb * 128 : orb * 128 + 128]
                for d in range(8):
                    at = h * 256 + orb * 128 + d * 16
                    m1[at : at + 16, lanes] = piece * dm[d, :, lanes]
    both = lax.dot_general(
        m1[...], lt[...], (((1,), (1,)), ((), ())), preferred_element_type=F32
    )
    both = both[:256] + both[256:]
    for hx in range(2):
        gs[hx] = both[:, hx * 128 : hx * 128 + 128]
    grid = [
        jnp.concatenate(
            [
                gs[hx, pl.ds(orb * 128 + c * 8 + z, 8, stride=16), :]
                for orb in range(2)
                for z in range(8)
                for c in range(2)
            ],
            axis=0,
        )
        for hx in range(2)
    ]

    def keep(value, at):
        high, low = halves(value)
        for orb in range(2):
            lanes = slice(orb * 128, orb * 128 + 128)
            bs[:, at : at + 16, lanes] = high[orb]
            bs[:, 80 + at : 96 + at, lanes] = high[orb]
            bs[:, 160 + at : 176 + at, lanes] = low[orb]

    loads[1].wait()
    for hx in range(2):
        high, low = halves(grid[hx])
        left = jnp.concatenate([high, high, low], axis=1)
        for i in range(2):
            turned = mm(left, wy[i]).reshape(2, 8, 2, 8, 256)
            real = turned[:, :, 0, :, :128] - turned[:, :, 1, :, 128:]
            imag = turned[:, :, 0, :, 128:] + turned[:, :, 1, :, :128]
            keep(jnp.concatenate([real, imag], axis=2), (2 * hx + i) * 16)
    keep(jnp.broadcast_to(grid[0][:, 31:32], (256, 128)).reshape(2, 8, 16, 128), 64)

    for k in range(1, n_y):
        gy_copy(k).wait_recv()
    loads[2].wait()
    loads[3].wait()

    for z in range(8):
        field = mm(xf[...], bs[z])
        plane = jnp.concatenate(
            [slab[b % n_y, b // n_y, z] for b in range(n_z * n_y)], axis=0
        )
        high, low = halves(field * jnp.concatenate([plane, plane], axis=1))
        back = mm(xb[...], jnp.concatenate([high, high, low], axis=0))
        for orb in range(2):
            lanes = slice(orb * 128, orb * 128 + 128)
            rows = slice(orb * 64 + z * 8, orb * 64 + z * 8 + 8)
            for xl in range(4):
                for c in range(2):
                    at = ((xl % 2) * 2 + c) * 128
                    cs[xl // 2, rows, at : at + 128] = back[
                        (xl * 2 + c) * 8 : (xl * 2 + c) * 8 + 8, lanes
                    ]
            for c in range(2):
                sp[c, rows, :] = back[64 + c * 8 : 72 + c * 8, lanes]

    loads[4].wait()
    at_zero = lax.broadcasted_iota(jnp.int32, (128, 128), 1) == 31
    for hx in range(2):
        high, low = halves(cs[hx])
        turned = mm(jnp.concatenate([high, high, low], axis=1), wb[...])
        for c in range(2):
            part = turned[:, c * 128 : c * 128 + 128]
            if hx == 0:
                part = part + jnp.where(at_zero, jnp.sum(sp[c], axis=1, keepdims=True), 0.0)
            og[hx, c * 128 : c * 128 + 128, :] = part

    picked = jnp.concatenate(
        [
            jnp.concatenate(
                [og[hx, pl.ds(c * 128 + d, 16, stride=8), :] for d in range(8) for c in range(2)],
                axis=0,
            )
            for hx in range(2)
        ],
        axis=1,
    )
    high, low = halves(picked)
    for n in range(8):
        chunk = lax.rem(me // 2 + n, 8)
        lanes = pl.ds(pl.multiple_of(chunk * 256, 256), 256)
        ones = lt[:, lanes]
        wide = (mm(high, ones) + mm(low, ones)).reshape(8, 32, 256)
        d_here = jnp.broadcast_to(sm_ref[0:1, lanes] & 7, (32, 256))
        total = wide[0]
        for d in range(1, 8):
            total = jnp.where(d_here == d, wide[d], total)
        for half in range(2):
            to = chunk * 2 + half
            for c in range(2):
                for orb in range(2):
                    s2[to, c * 8 : c * 8 + 8, orb * 128 : orb * 128 + 128] = total[
                        c * 16 + orb * 8 : c * 16 + orb * 8 + 8, half * 128 : half * 128 + 128
                    ]

            @pl.when(to != me)
            def _():
                b_copy(lax.rem(to - me + 16, 16)).start()

    r2[me] = s2[me]
    for k in range(1, 16):
        b_copy(k).wait_recv()

    high, low = halves(r2[...].reshape(256, 256))
    loads[5].wait()
    result = mm(zb[...], jnp.concatenate([high, high, low], axis=0)) * (2.0 / GRID**3)
    for orb in range(2):
        for c in range(2):
            o_ref[0, 2 * orb + c] = jnp.where(
                live, result[c * 72 : c * 72 + span, orb * 128 : orb * 128 + 128], 0.0
            )

    for k in range(1, n_z):
        gz_copy(k).wait_send()
    for k in range(1, n_y):
        gy_copy(k).wait_send()
    for k in range(1, 16):
        a_copy(k).wait_send()
        b_copy(k).wait_send()


def per_device(n_z, n_y, coeffs, potential, stick_map):
    consts = tables()
    vmem = pl.BlockSpec(memory_space=pltpu.VMEM)
    hbm = pl.BlockSpec(memory_space=pl.ANY)
    dma = pltpu.SemaphoreType.DMA
    scratch = [pltpu.VMEM(t.shape, BF) for t in consts] + [
        pltpu.VMEM((2, 80, 256), F32),
        pltpu.VMEM((16, 16, 256), F32),
        pltpu.VMEM((16, 16, 256), F32),
        pltpu.VMEM((16, 16, 256), F32),
        pltpu.VMEM((16, 16, 256), F32),
        pltpu.VMEM((n_y, n_z) + potential.shape, F32),
        pltpu.VMEM((256, 2048), BF),
        pltpu.VMEM((8, 16, 2048), BF),
        pltpu.VMEM((512, 2048), BF),
        pltpu.VMEM((2, 256, 128), F32),
        pltpu.VMEM((8, 240, 256), BF),
        pltpu.VMEM((2, 128, 512), F32),
        pltpu.VMEM((2, 128, 128), F32),
        pltpu.VMEM((2, 256, 128), F32),
        dma((len(consts),)),
        dma((16,)), dma((16,)), dma((16,)), dma((16,)),
        dma((4,)), dma((4,)), dma((4,)), dma((4,)), dma,
    ]
    return pl.pallas_call(
        functools.partial(kernel, n_z, n_y),
        out_shape=jax.ShapeDtypeStruct(coeffs.shape, F32),
        in_specs=[vmem, vmem, vmem] + [hbm] * len(consts),
        out_specs=vmem,
        scratch_shapes=scratch,
        compiler_params=pltpu.CompilerParams(
            collective_id=0, has_side_effects=True, vmem_limit_bytes=40 * 1024 * 1024
        ),
    )(coeffs, potential, stick_map, *[jnp.asarray(t) for t in consts])


def solution(mesh):
    n_band = mesh.shape["band"]
    n_z = 4 if n_band == 16 else 1
    placed = (P("band", None, None, "plane"), P("plane", "band", None), P())
    return jax.shard_map(
        functools.partial(per_device, n_z, n_band // n_z),
        mesh=mesh,
        in_specs=placed,
        out_specs=P("band", None, None, "plane"),
        check_vma=False,
    )
```

```python
import functools

import jax
import jax.numpy as jnp
import ml_dtypes
import numpy as np
from jax import lax
from jax.experimental import pallas as pl
from jax.experimental.pallas import tpu as pltpu
from jax.sharding import PartitionSpec as P

MESH = pl.DeviceIdType.MESH
GRID = 128
RADIUS = 32
BF = jnp.bfloat16
F32 = jnp.float32


def _halves(table):
    high = table.astype(ml_dtypes.bfloat16)
    low = (table - high.astype(np.float64)).astype(ml_dtypes.bfloat16)
    return high, low


def _left(table):
    high, low = _halves(table)
    return np.concatenate([high, low, high], axis=1)


def _right(table):
    high, low = _halves(table)
    return np.concatenate([high, low, high], axis=0)


def _trig(left, right):
    turns = np.mod(np.outer(left, right), GRID) * (2.0 * np.pi / GRID)
    return np.cos(turns), np.sin(turns)


def tables():
    points = np.arange(GRID)
    depth = np.arange(2 * RADIUS + 1) - RADIUS
    span = depth.size
    cos, sin = _trig(points, depth)
    zf = np.zeros((16, 2, 8, 2, 80))
    cos, sin = cos.reshape(16, 8, span), sin.reshape(16, 8, span)
    zf[:, 0, :, 0, :span], zf[:, 0, :, 1, :span] = cos, -sin
    zf[:, 1, :, 0, :span], zf[:, 1, :, 1, :span] = sin, cos
    zf = zf.reshape(16, 2, 2, 4, 160).transpose(2, 0, 1, 3, 4)
    zf = _left(zf.reshape(256, 160))
    zb = np.zeros((2, 72, 16, 2, 8))
    cos, sin = np.moveaxis(cos, 2, 0), np.moveaxis(sin, 2, 0)
    zb[0, :span, :, 0], zb[0, :span, :, 1] = cos, sin
    zb[1, :span, :, 0], zb[1, :span, :, 1] = -sin, cos
    zb = zb.reshape(144, 16, 2, 2, 4).transpose(0, 3, 1, 2, 4).reshape(144, 2, 128)
    zb = np.stack([_left(zb[:, h]) for h in range(2)])
    cos, sin = _trig(np.arange(64) - 31, points)
    wy = np.zeros((2, 2, 64, 2, GRID))
    wb = np.zeros((2, 2, GRID, 2, 2, 64))
    for i in range(2):
        wy[i, i, :, 0], wy[i, i, :, 1] = cos, sin
        wb[i, 0, :, 0, i], wb[i, 1, :, 0, i] = cos.T, sin.T
        wb[i, 0, :, 1, i], wb[i, 1, :, 1, i] = -sin.T, cos.T
    wy = np.stack([_right(wy[i].reshape(128, 256)) for i in range(2)])
    wb = _right(wb.reshape(512, 256))
    cos, sin = _trig(np.arange(32), points)
    base = np.zeros((5, 2, 8, GRID))
    base[:4, 0], base[:4, 1] = cos.reshape(4, 8, GRID), -sin.reshape(4, 8, GRID)
    cos, sin = _trig(np.array([RADIUS]), points)
    base[4, 0, 0], base[4, 1, 0] = cos[0] - 1.0, -sin[0]
    base = base.reshape(80, GRID)
    xf, xb = _left(base.T), _left(base)
    return zf, wy, xf, xb, wb, zb


def halves(value):
    high = value.astype(BF)
    return high, (value - high.astype(F32)).astype(BF)


def mm(left, right):
    return jnp.dot(left, right, preferred_element_type=F32)


OFFSETS = [(dx, dz, dc) for dz in (1, 0) for dx in (2, 1, 3, 0) for dc in (1, 0)]
PEERS = [o for o in OFFSETS if o != (0, 0, 0)]
CHUNKS = [o for o in OFFSETS if o[2] == 0]


def kernel(
    n_z, n_y,
    c_h, p_h, sm_h, zf_h, wy_h, xf_h, xb_h, wb_h, zb_h,
    o_ref,
    c_ref, sm_ref, zf, wy, xf, xb, wb, zb,
    xs, zs, r1, s2, r2, slab, lt, dm, m1, gs, bs, cs, sp, og,
    c_sem, a_s, a_r, b_s, b_r, gz_s, gz_r, gy_s, gy_r, own_sem,
):
    band = lax.axis_index("band")
    me = lax.axis_index("plane")
    z_me, y_me = band // n_y, lax.rem(band, n_y)
    x_at, half_at, core_at = me // 4, lax.rem(me // 2, 2), lax.rem(me, 2)
    span = c_ref.shape[0]

    def plane_peer(offset, sign=1):
        dx, dz, dc = offset
        return (
            lax.rem(x_at + sign * dx + 4, 4) * 4
            + lax.rem(half_at + dz, 2) * 2
            + lax.rem(core_at + dc, 2)
        )

    def z_peer(k):
        return lax.rem(z_me + k, n_z) * n_y + y_me

    def y_peer(k):
        return z_me * n_y + lax.rem(y_me + k, n_y)

    barrier = pltpu.get_barrier_semaphore()
    for o in PEERS:
        pl.semaphore_signal(
            barrier, inc=1, device_id={"plane": plane_peer(o)}, device_id_type=MESH
        )
    for k in range(1, n_z):
        pl.semaphore_signal(barrier, inc=1, device_id={"band": z_peer(k)}, device_id_type=MESH)
    for k in range(1, n_y):
        pl.semaphore_signal(barrier, inc=1, device_id={"band": y_peer(k)}, device_id_type=MESH)

    loads = [
        pltpu.make_async_copy(src, dst, c_sem.at[n])
        for n, (src, dst) in enumerate(
            [
                (c_h, c_ref), (sm_h, sm_ref), (zf_h, zf), (wy_h, wy),
                (xf_h, xf), (xb_h, xb), (wb_h, wb), (zb_h, zb),
            ]
        )
    ]
    for load in loads[:3]:
        load.start()

    def a_copy(h, n):
        to = plane_peer(PEERS[n])
        return pltpu.make_async_remote_copy(
            src_ref=zs.at[h, to], dst_ref=r1.at[h, me],
            send_sem=a_s.at[h, n], recv_sem=a_r.at[h, n],
            device_id={"plane": to}, device_id_type=MESH,
        )

    def b_copy(h, n):
        to = plane_peer(PEERS[n])
        return pltpu.make_async_remote_copy(
            src_ref=s2.at[h, to], dst_ref=r2.at[h, me],
            send_sem=b_s.at[h, n], recv_sem=b_r.at[h, n],
            device_id={"plane": to}, device_id_type=MESH,
        )

    def gz_copy(h, k):
        return pltpu.make_async_remote_copy(
            src_ref=p_h.at[pl.ds(h * 4, 4)], dst_ref=slab.at[h, y_me, z_me],
            send_sem=gz_s.at[h, k], recv_sem=gz_r.at[h, k],
            device_id={"band": z_peer(k)}, device_id_type=MESH,
        )

    def gy_copy(h, back, k):
        z_from = lax.rem(z_me - back + n_z, n_z)
        own = p_h.at[pl.ds(h * 4, 4)]
        return pltpu.make_async_remote_copy(
            src_ref=slab.at[h, y_me, z_from] if back else own, dst_ref=slab.at[h, y_me, z_from],
            send_sem=gy_s.at[h, back, k], recv_sem=gy_r.at[h, back, k],
            device_id={"band": y_peer(k)}, device_id_type=MESH,
        )

    def own_copy(h):
        return pltpu.make_async_copy(
            p_h.at[pl.ds(h * 4, 4)], slab.at[h, y_me, z_me], own_sem.at[h]
        )

    def gather_start(h):
        for k in range(1, n_z):
            gz_copy(h, k).start()
        for k in range(1, n_y):
            gy_copy(h, 0, k).start()

    pl.semaphore_wait(barrier, 15 + n_z - 1 + n_y - 1)
    gather_start(0)

    loads[0].wait()
    loads[1].wait()
    heights = sm_ref[2:3, pl.ds(pl.multiple_of(me * 128, 128), 128)]
    live = jnp.abs(lax.broadcasted_iota(jnp.int32, (span, 128), 0) - RADIUS) <= heights
    xs[:, 64:80, :] = jnp.zeros((2, 16, 256), F32)
    for orb in range(2):
        for c in range(2):
            xs[c, 0:span, orb * 128 : orb * 128 + 128] = jnp.where(
                live, c_ref[:, 2 * orb + c, :], 0.0
            )
    high, low = halves(xs[...].reshape(160, 256))
    stacked = jnp.concatenate([high, high, low], axis=0)
    loads[2].wait()
    for h in range(2):
        zs[h] = mm(zf[h * 128 : h * 128 + 128], stacked).reshape(16, 8, 256)
        for n in range(15):
            a_copy(h, n).start()
        if h == 0:
            gather_start(1)
    for load in loads[3:]:
        load.start()
    for h in range(2):
        own_copy(h).start()
        r1[h, me] = zs[h, me]

    stick_x, stick_y = sm_ref[0:1, :], sm_ref[1:2, :]
    d_of = stick_x & 7
    lane_of = ((stick_x >> 3) & 3) * 64 + stick_y + 31
    for n in range(16):
        rows = lax.broadcasted_iota(jnp.int32, (16, 2048), 0) + n * 16
        lt[n * 16 : n * 16 + 16, :] = jnp.where(rows == lane_of, 1.0, 0.0).astype(BF)
    for n in range(4):
        rows = lax.broadcasted_iota(jnp.int32, (16, 2048), 0) // 8 + n * 2
        dm[n] = jnp.where(rows == d_of, 1.0, 0.0).astype(BF)

    for h in range(2):
        for back in sorted(range(1, n_z), key=lambda k: min(k, n_z - k)):
            gz_copy(h, back).wait_recv()
            for k in range(1, n_y):
                gy_copy(h, back, k).start()

    at_zero = lax.broadcasted_iota(jnp.int32, (64, 128), 1) == 31

    def place(h, source):
        lanes = pl.ds(pl.multiple_of(source * 128, 128), 128)
        block = r1[h, source]
        twice = jnp.concatenate([block, block], axis=0)
        for p, part in enumerate(halves(twice)):
            for orb in range(2):
                piece = part[:, orb * 128 : orb * 128 + 128]
                for n in range(4):
                    at = p * 128 + orb * 64 + n * 16
                    m1[h, at : at + 16, lanes] = piece * dm[n, :, lanes]

    def keep(h, value, at):
        high, low = halves(value)
        for orb in range(2):
            lanes = slice(orb * 128, orb * 128 + 128)
            bs[h, :, at : at + 16, lanes] = high[orb]
            bs[h, :, 80 + at : 96 + at, lanes] = high[orb]
            bs[h, :, 160 + at : 176 + at, lanes] = low[orb]

    def middle(h):
        place(h, me)
        for n in reversed(range(15)):
            a_copy(h, n).wait_recv()
            place(h, plane_peer(PEERS[n], -1))
        both = lax.dot_general(
            m1[h], lt[...], (((1,), (1,)), ((), ())), preferred_element_type=F32
        )
        both = both[:128] + both[128:]
        for hx in range(2):
            gs[h, hx] = both[:, hx * 128 : hx * 128 + 128]
        grid = [
            jnp.concatenate(
                [
                    gs[h, hx, pl.ds(orb * 64 + c * 4 + z, 8, stride=8), :]
                    for orb in range(2)
                    for z in range(4)
                    for c in range(2)
                ],
                axis=0,
            )
            for hx in range(2)
        ]

        if h == 0:
            loads[3].wait()
        for hx in range(2):
            high, low = halves(grid[hx])
            left = jnp.concatenate([high, high, low], axis=1)
            for i in range(2):
                turned = mm(left, wy[i]).reshape(2, 4, 2, 8, 256)
                real = turned[:, :, 0, :, :128] - turned[:, :, 1, :, 128:]
                imag = turned[:, :, 0, :, 128:] + turned[:, :, 1, :, :128]
                keep(h, jnp.concatenate([real, imag], axis=2), (2 * hx + i) * 16)
        keep(h, jnp.broadcast_to(grid[0][:, 31:32], (128, 128)).reshape(2, 4, 16, 128), 64)

        own_copy(h).wait()
        for back in range(n_z):
            for k in range(1, n_y):
                gy_copy(h, back, k).wait_recv()
        if h == 0:
            loads[4].wait()
            loads[5].wait()

        for z in range(4):
            field = mm(xf[...], bs[h, z])
            plane = jnp.concatenate(
                [slab[h, b % n_y, b // n_y, z] for b in range(n_z * n_y)], axis=0
            )
            high, low = halves(field * jnp.concatenate([plane, plane], axis=1))
            back = mm(xb[...], jnp.concatenate([high, high, low], axis=0))
            for orb in range(2):
                lanes = slice(orb * 128, orb * 128 + 128)
                rows = slice(orb * 32 + z * 8, orb * 32 + z * 8 + 8)
                for xl in range(4):
                    for c in range(2):
                        at = ((xl % 2) * 2 + c) * 128
                        cs[h, xl // 2, rows, at : at + 128] = back[
                            (xl * 2 + c) * 8 : (xl * 2 + c) * 8 + 8, lanes
                        ]
                for c in range(2):
                    sp[h, c, rows, :] = back[64 + c * 8 : 72 + c * 8, lanes]

        if h == 0:
            loads[6].wait()
        for hx in range(2):
            high, low = halves(cs[h, hx])
            turned = mm(jnp.concatenate([high, high, low], axis=1), wb[...])
            for c in range(2):
                part = turned[:, c * 128 : c * 128 + 128]
                if hx == 0:
                    extra = jnp.sum(sp[h, c], axis=1, keepdims=True)
                    part = part + jnp.where(at_zero, extra, 0.0)
                for orb in range(2):
                    at = orb * 64 + c * 32
                    og[h, hx, at : at + 32, :] = part[orb * 32 : orb * 32 + 32]

        picked = jnp.concatenate(
            [
                jnp.concatenate(
                    [
                        og[h, hx, pl.ds(orb * 64 + d, 8, stride=8), :]
                        for d in range(8)
                        for orb in range(2)
                    ],
                    axis=0,
                )
                for hx in range(2)
            ],
            axis=1,
        )
        high, low = halves(picked)
        for chunk_offset in CHUNKS:
            chunk = plane_peer(chunk_offset) // 2
            lanes = pl.ds(pl.multiple_of(chunk * 256, 256), 256)
            ones = lt[:, lanes]
            wide = (mm(high, ones) + mm(low, ones)).reshape(8, 16, 256)
            d_here = jnp.broadcast_to(sm_ref[0:1, lanes] & 7, (16, 256))
            total = wide[0]
            for d in range(1, 8):
                total = jnp.where(d_here == d, wide[d], total)
            for core in range(2):
                for orb in range(2):
                    s2[h, chunk * 2 + core, :, orb * 128 : orb * 128 + 128] = total[
                        orb * 8 : orb * 8 + 8, core * 128 : core * 128 + 128
                    ]
            for n, o in enumerate(PEERS):
                if o[:2] == chunk_offset[:2]:
                    b_copy(h, n).start()
        r2[h, me] = s2[h, me]

    middle(0)
    middle(1)

    for h in range(2):
        for k in range(1, n_z):
            gz_copy(h, k).wait_send()
        for back in range(n_z):
            for k in range(1, n_y):
                gy_copy(h, back, k).wait_send()
        for n in range(15):
            a_copy(h, n).wait_send()
    loads[7].wait()
    result = None
    for h in range(2):
        for n in range(15):
            b_copy(h, n).wait_send()
        for n in range(15):
            b_copy(h, n).wait_recv()
        high, low = halves(r2[h].reshape(128, 256))
        part = mm(zb[h], jnp.concatenate([high, high, low], axis=0))
        result = part if h == 0 else result + part
    result = result * (2.0 / GRID**3)
    for orb in range(2):
        for c in range(2):
            o_ref[:, 2 * orb + c, :] = jnp.where(
                live, result[c * 72 : c * 72 + span, orb * 128 : orb * 128 + 128], 0.0
            )


def per_device(n_z, n_y, coeffs, potential, stick_map):
    consts = tables()
    moved = jnp.transpose(coeffs[0], (1, 0, 2))
    vmem = pl.BlockSpec(memory_space=pltpu.VMEM)
    hbm = pl.BlockSpec(memory_space=pltpu.HBM)
    dma = pltpu.SemaphoreType.DMA
    scratch = [
        pltpu.VMEM(moved.shape, F32),
        pltpu.VMEM(stick_map.shape, jnp.int32),
    ] + [pltpu.VMEM(t.shape, BF) for t in consts] + [
        pltpu.VMEM((2, 80, 256), F32),
        pltpu.VMEM((2, 16, 8, 256), F32),
        pltpu.VMEM((2, 16, 8, 256), F32),
        pltpu.VMEM((2, 16, 8, 256), F32),
        pltpu.VMEM((2, 16, 8, 256), F32),
        pltpu.VMEM((2, n_y, n_z, 4) + potential.shape[1:], F32),
        pltpu.VMEM((256, 2048), BF),
        pltpu.VMEM((4, 16, 2048), BF),
        pltpu.VMEM((2, 256, 2048), BF),
        pltpu.VMEM((2, 2, 128, 128), F32),
        pltpu.VMEM((2, 4, 240, 256), BF),
        pltpu.VMEM((2, 2, 64, 512), F32),
        pltpu.VMEM((2, 2, 64, 128), F32),
        pltpu.VMEM((2, 2, 128, 128), F32),
        dma((len(consts) + 2,)),
        dma((2, 16)), dma((2, 16)), dma((2, 16)), dma((2, 16)),
        dma((2, 4)), dma((2, 4)), dma((2, 4, 4)), dma((2, 4, 4)), dma((2,)),
    ]
    result = pl.pallas_call(
        functools.partial(kernel, n_z, n_y),
        out_shape=jax.ShapeDtypeStruct(moved.shape, F32),
        in_specs=[hbm] * (len(consts) + 3),
        out_specs=vmem,
        scratch_shapes=scratch,
        compiler_params=pltpu.CompilerParams(
            collective_id=0, has_side_effects=True, vmem_limit_bytes=40 * 1024 * 1024
        ),
    )(
        *[
            pltpu.with_memory_space_constraint(value, pltpu.HBM)
            for value in (moved, potential, stick_map, *[jnp.asarray(t) for t in consts])
        ]
    )
    return jnp.transpose(result, (1, 0, 2))[None]


def solution(mesh):
    n_band = mesh.shape["band"]
    n_z = 4 if n_band == 16 else 1
    placed = (P("band", None, None, "plane"), P("plane", "band", None), P())
    return jax.shard_map(
        functools.partial(per_device, n_z, n_band // n_z),
        mesh=mesh,
        in_specs=placed,
        out_specs=P("band", None, None, "plane"),
        check_vma=False,
    )
```

```python
import functools

import jax
import jax.numpy as jnp
import ml_dtypes
import numpy as np
from jax import lax
from jax.experimental import pallas as pl
from jax.experimental.pallas import tpu as pltpu
from jax.sharding import PartitionSpec as P

MESH = pl.DeviceIdType.MESH
GRID = 128
RADIUS = 32
BF = jnp.bfloat16
F32 = jnp.float32


def _halves(table):
    high = table.astype(ml_dtypes.bfloat16)
    low = (table - high.astype(np.float64)).astype(ml_dtypes.bfloat16)
    return high, low


def _left(table):
    high, low = _halves(table)
    return np.concatenate([high, low, high], axis=1)


def _right(table):
    high, low = _halves(table)
    return np.concatenate([high, low, high], axis=0)


def _trig(left, right):
    turns = np.mod(np.outer(left, right), GRID) * (2.0 * np.pi / GRID)
    return np.cos(turns), np.sin(turns)


def tables():
    points = np.arange(GRID)
    depth = np.arange(2 * RADIUS + 1) - RADIUS
    span = depth.size
    cos, sin = _trig(points, depth)
    zf = np.zeros((16, 2, 8, 2, 80))
    cos, sin = cos.reshape(16, 8, span), sin.reshape(16, 8, span)
    zf[:, 0, :, 0, :span], zf[:, 0, :, 1, :span] = cos, -sin
    zf[:, 1, :, 0, :span], zf[:, 1, :, 1, :span] = sin, cos
    zf = zf.reshape(16, 2, 2, 4, 160).transpose(2, 0, 1, 3, 4)
    zf = _left(zf.reshape(256, 160))
    zb = np.zeros((2, 72, 16, 2, 8))
    cos, sin = np.moveaxis(cos, 2, 0), np.moveaxis(sin, 2, 0)
    zb[0, :span, :, 0], zb[0, :span, :, 1] = cos, sin
    zb[1, :span, :, 0], zb[1, :span, :, 1] = -sin, cos
    zb = zb.reshape(144, 16, 2, 2, 4).transpose(0, 3, 1, 2, 4).reshape(144, 2, 128)
    zb = np.stack([_left(zb[:, h]) for h in range(2)])
    cos, sin = _trig(np.arange(64) - 31, points)
    wy = np.zeros((2, 2, 64, 2, GRID))
    wb = np.zeros((2, 2, GRID, 2, 2, 64))
    for i in range(2):
        wy[i, i, :, 0], wy[i, i, :, 1] = cos, sin
        wb[i, 0, :, 0, i], wb[i, 1, :, 0, i] = cos.T, sin.T
        wb[i, 0, :, 1, i], wb[i, 1, :, 1, i] = -sin.T, cos.T
    wy = np.stack([_right(wy[i].reshape(128, 256)) for i in range(2)])
    wb = _right(wb.reshape(512, 256))
    cos, sin = _trig(np.arange(32), points)
    base = np.zeros((5, 2, 8, GRID))
    base[:4, 0], base[:4, 1] = cos.reshape(4, 8, GRID), -sin.reshape(4, 8, GRID)
    cos, sin = _trig(np.array([RADIUS]), points)
    base[4, 0, 0], base[4, 1, 0] = cos[0] - 1.0, -sin[0]
    base = base.reshape(80, GRID)
    xf, xb = _left(base.T), _left(base)
    return zf, wy, xf, xb, wb, zb


def halves(value):
    high = value.astype(BF)
    return high, (value - high.astype(F32)).astype(BF)


def mm(left, right):
    return jnp.dot(left, right, preferred_element_type=F32)


OFFSETS = [(dx, dz, dc) for dz in (1, 0) for dx in (2, 1, 3, 0) for dc in (1, 0)]
CHUNKS = [o for o in OFFSETS if o[2] == 0]


def kernel(
    n_z, n_y,
    c_h, p_h, sm_h, zf_h, wy_h, xf_h, xb_h, wb_h, zb_h,
    o_ref,
    c_ref, sm_ref, zf, wy, xf, xb, wb, zb,
    xs, zs, r1, s2, r2, slab, lt, dm, m1, gs, bs, cs, sp, og,
    c_sem, a_s, a_r, b_s, b_r, gz_s, gz_r, gy_s, gy_r, own_sem,
):
    band = lax.axis_index("band")
    me = lax.axis_index("plane")
    z_me, y_me = band // n_y, lax.rem(band, n_y)
    x_at, half_at, core_at = me // 4, lax.rem(me // 2, 2), lax.rem(me, 2)
    span = c_ref.shape[0]

    def plane_peer(offset, sign=1):
        dx, dz, dc = offset
        return (
            lax.rem(x_at + sign * dx + 4, 4) * 4
            + lax.rem(half_at + dz, 2) * 2
            + lax.rem(core_at + dc, 2)
        )

    side = lax.rem(z_me, 2)
    partner = [
        lax.rem(z_me + 2, n_z) * n_y + y_me,
        (z_me + 1 - 2 * side) * n_y + y_me,
    ]
    half_of = [side, 1 - side]

    def z_peer(k):
        return lax.rem(z_me + k, n_z) * n_y + y_me

    def y_peer(k):
        return z_me * n_y + lax.rem(y_me + k, n_y)

    loads = [
        pltpu.make_async_copy(src, dst, c_sem.at[n])
        for n, (src, dst) in enumerate(
            [
                (c_h, c_ref), (sm_h, sm_ref), (zf_h, zf), (wy_h, wy),
                (xf_h, xf), (xb_h, xb), (wb_h, wb), (zb_h, zb),
            ]
        )
    ]
    for load in loads[:3]:
        load.start()

    barrier = pltpu.get_barrier_semaphore()
    for band_to in partner:
        for o in OFFSETS:
            pl.semaphore_signal(
                barrier, inc=1,
                device_id={"band": band_to, "plane": plane_peer(o)}, device_id_type=MESH,
            )
    last = lax.rem(z_me + 3 - 2 * side + n_z, n_z) * n_y + y_me
    pl.semaphore_signal(barrier, inc=1, device_id={"band": last}, device_id_type=MESH)
    for k in range(1, n_y):
        pl.semaphore_signal(barrier, inc=1, device_id={"band": y_peer(k)}, device_id_type=MESH)

    def a_copy(h, n):
        to = plane_peer(OFFSETS[n])
        return pltpu.make_async_remote_copy(
            src_ref=zs.at[half_of[h], to], dst_ref=r1.at[h, me],
            send_sem=a_s.at[h, n], recv_sem=a_r.at[h, n],
            device_id={"band": partner[h], "plane": to}, device_id_type=MESH,
        )

    def b_copy(h, n):
        to = plane_peer(OFFSETS[n])
        return pltpu.make_async_remote_copy(
            src_ref=s2.at[h, to], dst_ref=r2.at[side, me],
            send_sem=b_s.at[h, n], recv_sem=b_r.at[h, n],
            device_id={"band": partner[h], "plane": to}, device_id_type=MESH,
        )

    def gz_copy(k):
        at = lax.rem(z_me + k, 2) * 4
        return pltpu.make_async_remote_copy(
            src_ref=p_h.at[pl.ds(at, 4)], dst_ref=slab.at[y_me, z_me],
            send_sem=gz_s.at[k], recv_sem=gz_r.at[k],
            device_id={"band": z_peer(k)}, device_id_type=MESH,
        )

    def gy_copy(back, k):
        z_from = lax.rem(z_me - back + n_z, n_z)
        own = p_h.at[pl.ds(side * 4, 4)]
        return pltpu.make_async_remote_copy(
            src_ref=slab.at[y_me, z_from] if back else own, dst_ref=slab.at[y_me, z_from],
            send_sem=gy_s.at[back, k], recv_sem=gy_r.at[back, k],
            device_id={"band": y_peer(k)}, device_id_type=MESH,
        )

    own_copy = pltpu.make_async_copy(
        p_h.at[pl.ds(side * 4, 4)], slab.at[y_me, z_me], own_sem
    )

    pl.semaphore_wait(barrier, 33 + n_y - 1)
    for k in range(1, n_z):
        gz_copy(k).start()
    for k in range(1, n_y):
        gy_copy(0, k).start()

    loads[0].wait()
    loads[1].wait()
    heights = sm_ref[2:3, pl.ds(pl.multiple_of(me * 128, 128), 128)]
    live = jnp.abs(lax.broadcasted_iota(jnp.int32, (span, 128), 0) - RADIUS) <= heights
    xs[:, 64:80, :] = jnp.zeros((2, 16, 256), F32)
    for orb in range(2):
        for c in range(2):
            xs[c, 0:span, orb * 128 : orb * 128 + 128] = jnp.where(
                live, c_ref[:, 2 * orb + c, :], 0.0
            )
    high, low = halves(xs[...].reshape(160, 256))
    stacked = jnp.concatenate([high, high, low], axis=0)
    loads[2].wait()
    for h in range(2):
        zs[half_of[h]] = mm(
            zf[pl.ds(pl.multiple_of(half_of[h] * 128, 128), 128), :], stacked
        ).reshape(16, 8, 256)
        for n in range(16):
            a_copy(h, n).start()
    for load in loads[3:]:
        load.start()
    own_copy.start()

    stick_x, stick_y = sm_ref[0:1, :], sm_ref[1:2, :]
    d_of = stick_x & 7
    lane_of = ((stick_x >> 3) & 3) * 64 + stick_y + 31
    for n in range(16):
        rows = lax.broadcasted_iota(jnp.int32, (16, 2048), 0) + n * 16
        lt[n * 16 : n * 16 + 16, :] = jnp.where(rows == lane_of, 1.0, 0.0).astype(BF)
    for n in range(4):
        rows = lax.broadcasted_iota(jnp.int32, (16, 2048), 0) // 8 + n * 2
        dm[n] = jnp.where(rows == d_of, 1.0, 0.0).astype(BF)

    for back in sorted(range(1, n_z), key=lambda k: min(k, n_z - k)):
        gz_copy(back).wait_recv()
        for k in range(1, n_y):
            gy_copy(back, k).start()

    at_zero = lax.broadcasted_iota(jnp.int32, (64, 128), 1) == 31

    def place(h, source):
        lanes = pl.ds(pl.multiple_of(source * 128, 128), 128)
        block = r1[h, source]
        twice = jnp.concatenate([block, block], axis=0)
        for p, part in enumerate(halves(twice)):
            for orb in range(2):
                piece = part[:, orb * 128 : orb * 128 + 128]
                for n in range(4):
                    at = p * 128 + orb * 64 + n * 16
                    m1[h, at : at + 16, lanes] = piece * dm[n, :, lanes]

    def keep(h, value, at):
        high, low = halves(value)
        for orb in range(2):
            lanes = slice(orb * 128, orb * 128 + 128)
            bs[h, :, at : at + 16, lanes] = high[orb]
            bs[h, :, 80 + at : 96 + at, lanes] = high[orb]
            bs[h, :, 160 + at : 176 + at, lanes] = low[orb]

    def to_columns(h):
        for n in reversed(range(16)):
            a_copy(h, n).wait_recv()
            place(h, plane_peer(OFFSETS[n], -1))
        both = lax.dot_general(
            m1[h], lt[...], (((1,), (1,)), ((), ())), preferred_element_type=F32
        )
        both = both[:128] + both[128:]
        for hx in range(2):
            gs[h, hx] = both[:, hx * 128 : hx * 128 + 128]
        grid = [
            jnp.concatenate(
                [
                    gs[h, hx, pl.ds(orb * 64 + c * 4 + z, 8, stride=8), :]
                    for orb in range(2)
                    for z in range(4)
                    for c in range(2)
                ],
                axis=0,
            )
            for hx in range(2)
        ]

        if h == 0:
            loads[3].wait()
        for hx in range(2):
            high, low = halves(grid[hx])
            left = jnp.concatenate([high, high, low], axis=1)
            for i in range(2):
                turned = mm(left, wy[i]).reshape(2, 4, 2, 8, 256)
                real = turned[:, :, 0, :, :128] - turned[:, :, 1, :, 128:]
                imag = turned[:, :, 0, :, 128:] + turned[:, :, 1, :, :128]
                keep(h, jnp.concatenate([real, imag], axis=2), (2 * hx + i) * 16)
        keep(h, jnp.broadcast_to(grid[0][:, 31:32], (128, 128)).reshape(2, 4, 16, 128), 64)

    def through_planes(h):
        if h == 0:
            own_copy.wait()
            for back in range(n_z):
                for k in range(1, n_y):
                    gy_copy(back, k).wait_recv()
            loads[4].wait()
            loads[5].wait()

        for z in range(4):
            field = mm(xf[...], bs[h, z])
            plane = jnp.concatenate(
                [slab[b % n_y, b // n_y, z] for b in range(n_z * n_y)], axis=0
            )
            high, low = halves(field * jnp.concatenate([plane, plane], axis=1))
            back = mm(xb[...], jnp.concatenate([high, high, low], axis=0))
            for orb in range(2):
                lanes = slice(orb * 128, orb * 128 + 128)
                rows = slice(orb * 32 + z * 8, orb * 32 + z * 8 + 8)
                for xl in range(4):
                    for c in range(2):
                        at = ((xl % 2) * 2 + c) * 128
                        cs[h, xl // 2, rows, at : at + 128] = back[
                            (xl * 2 + c) * 8 : (xl * 2 + c) * 8 + 8, lanes
                        ]
                for c in range(2):
                    sp[h, c, rows, :] = back[64 + c * 8 : 72 + c * 8, lanes]

        if h == 0:
            loads[6].wait()
        for hx in range(2):
            high, low = halves(cs[h, hx])
            turned = mm(jnp.concatenate([high, high, low], axis=1), wb[...])
            for c in range(2):
                part = turned[:, c * 128 : c * 128 + 128]
                if hx == 0:
                    extra = jnp.sum(sp[h, c], axis=1, keepdims=True)
                    part = part + jnp.where(at_zero, extra, 0.0)
                for orb in range(2):
                    at = orb * 64 + c * 32
                    og[h, hx, at : at + 32, :] = part[orb * 32 : orb * 32 + 32]

        picked = jnp.concatenate(
            [
                jnp.concatenate(
                    [
                        og[h, hx, pl.ds(orb * 64 + d, 8, stride=8), :]
                        for d in range(8)
                        for orb in range(2)
                    ],
                    axis=0,
                )
                for hx in range(2)
            ],
            axis=1,
        )
        high, low = halves(picked)
        for chunk_offset in CHUNKS:
            chunk = plane_peer(chunk_offset) // 2
            lanes = pl.ds(pl.multiple_of(chunk * 256, 256), 256)
            ones = lt[:, lanes]
            wide = (mm(high, ones) + mm(low, ones)).reshape(8, 16, 256)
            d_here = jnp.broadcast_to(sm_ref[0:1, lanes] & 7, (16, 256))
            total = wide[0]
            for d in range(1, 8):
                total = jnp.where(d_here == d, wide[d], total)
            for core in range(2):
                for orb in range(2):
                    s2[h, chunk * 2 + core, :, orb * 128 : orb * 128 + 128] = total[
                        orb * 8 : orb * 8 + 8, core * 128 : core * 128 + 128
                    ]
            for n, o in enumerate(OFFSETS):
                if o[:2] == chunk_offset[:2]:
                    b_copy(h, n).start()

    to_columns(0)
    to_columns(1)
    through_planes(0)
    through_planes(1)

    for k in range(1, n_z):
        gz_copy(k).wait_send()
    for back in range(n_z):
        for k in range(1, n_y):
            gy_copy(back, k).wait_send()
    for h in range(2):
        for n in range(16):
            a_copy(h, n).wait_send()
    loads[7].wait()
    result = None
    for h in range(2):
        for n in range(16):
            b_copy(h, n).wait_send()
        for n in range(16):
            b_copy(h, n).wait_recv()
        high, low = halves(r2[half_of[h]].reshape(128, 256))
        part = mm(zb[half_of[h]], jnp.concatenate([high, high, low], axis=0))
        result = part if h == 0 else result + part
    result = result * (2.0 / GRID**3)
    for orb in range(2):
        for c in range(2):
            o_ref[:, 2 * orb + c, :] = jnp.where(
                live, result[c * 72 : c * 72 + span, orb * 128 : orb * 128 + 128], 0.0
            )


def per_device(n_z, n_y, coeffs, potential, stick_map):
    consts = tables()
    moved = jnp.transpose(coeffs[0], (1, 0, 2))
    vmem = pl.BlockSpec(memory_space=pltpu.VMEM)
    hbm = pl.BlockSpec(memory_space=pltpu.HBM)
    dma = pltpu.SemaphoreType.DMA
    scratch = [
        pltpu.VMEM(moved.shape, F32),
        pltpu.VMEM(stick_map.shape, jnp.int32),
    ] + [pltpu.VMEM(t.shape, BF) for t in consts] + [
        pltpu.VMEM((2, 80, 256), F32),
        pltpu.VMEM((2, 16, 8, 256), F32),
        pltpu.VMEM((2, 16, 8, 256), F32),
        pltpu.VMEM((2, 16, 8, 256), F32),
        pltpu.VMEM((2, 16, 8, 256), F32),
        pltpu.VMEM((n_y, n_z, 4) + potential.shape[1:], F32),
        pltpu.VMEM((256, 2048), BF),
        pltpu.VMEM((4, 16, 2048), BF),
        pltpu.VMEM((2, 256, 2048), BF),
        pltpu.VMEM((2, 2, 128, 128), F32),
        pltpu.VMEM((2, 4, 240, 256), BF),
        pltpu.VMEM((2, 2, 64, 512), F32),
        pltpu.VMEM((2, 2, 64, 128), F32),
        pltpu.VMEM((2, 2, 128, 128), F32),
        dma((len(consts) + 2,)),
        dma((2, 16)), dma((2, 16)), dma((2, 16)), dma((2, 16)),
        dma((4,)), dma((4,)), dma((4, 4)), dma((4, 4)), dma,
    ]
    result = pl.pallas_call(
        functools.partial(kernel, n_z, n_y),
        out_shape=jax.ShapeDtypeStruct(moved.shape, F32),
        in_specs=[hbm] * (len(consts) + 3),
        out_specs=vmem,
        scratch_shapes=scratch,
        compiler_params=pltpu.CompilerParams(
            collective_id=0, has_side_effects=True, vmem_limit_bytes=40 * 1024 * 1024
        ),
    )(
        *[
            pltpu.with_memory_space_constraint(value, pltpu.HBM)
            for value in (moved, potential, stick_map, *[jnp.asarray(t) for t in consts])
        ]
    )
    return jnp.transpose(result, (1, 0, 2))[None]


def solution(mesh):
    n_band = mesh.shape["band"]
    n_z = 4 if n_band == 16 else 1
    placed = (P("band", None, None, "plane"), P("plane", "band", None), P())
    return jax.shard_map(
        functools.partial(per_device, n_z, n_band // n_z),
        mesh=mesh,
        in_specs=placed,
        out_specs=P("band", None, None, "plane"),
        check_vma=False,
    )
```

```python
import functools

import jax
import jax.numpy as jnp
import ml_dtypes
import numpy as np
from jax import lax
from jax.experimental import pallas as pl
from jax.experimental.pallas import tpu as pltpu
from jax.sharding import PartitionSpec as P

MESH = pl.DeviceIdType.MESH
GRID = 128
RADIUS = 32
BF = jnp.bfloat16
F32 = jnp.float32


def _halves(table):
    high = table.astype(ml_dtypes.bfloat16)
    low = (table - high.astype(np.float64)).astype(ml_dtypes.bfloat16)
    return high, low


def _left(table):
    high, low = _halves(table)
    return np.concatenate([high, low, high], axis=1)


def _right(table):
    high, low = _halves(table)
    return np.concatenate([high, low, high], axis=0)


def _trig(left, right):
    turns = np.mod(np.outer(left, right), GRID) * (2.0 * np.pi / GRID)
    return np.cos(turns), np.sin(turns)


def tables():
    points = np.arange(GRID)
    depth = np.arange(2 * RADIUS + 1) - RADIUS
    span = depth.size
    cos, sin = _trig(points, depth)
    zf = np.zeros((16, 2, 8, 2, 80))
    cos, sin = cos.reshape(16, 8, span), sin.reshape(16, 8, span)
    zf[:, 0, :, 0, :span], zf[:, 0, :, 1, :span] = cos, -sin
    zf[:, 1, :, 0, :span], zf[:, 1, :, 1, :span] = sin, cos
    zf = zf.reshape(16, 2, 2, 4, 160).transpose(2, 0, 1, 3, 4)
    zf = _left(zf.reshape(256, 160))
    zb = np.zeros((2, 72, 16, 2, 8))
    cos, sin = np.moveaxis(cos, 2, 0), np.moveaxis(sin, 2, 0)
    zb[0, :span, :, 0], zb[0, :span, :, 1] = cos, sin
    zb[1, :span, :, 0], zb[1, :span, :, 1] = -sin, cos
    zb = zb.reshape(144, 16, 2, 2, 4).transpose(0, 3, 1, 2, 4).reshape(144, 2, 128)
    zb = np.stack([_left(zb[:, h]) for h in range(2)])
    cos, sin = _trig(np.arange(64) - 31, points)
    wy = np.zeros((2, 2, 64, 2, GRID))
    wb = np.zeros((2, 2, GRID, 2, 2, 64))
    for i in range(2):
        wy[i, i, :, 0], wy[i, i, :, 1] = cos, sin
        wb[i, 0, :, 0, i], wb[i, 1, :, 0, i] = cos.T, sin.T
        wb[i, 0, :, 1, i], wb[i, 1, :, 1, i] = -sin.T, cos.T
    wy = np.stack([_right(wy[i].reshape(128, 256)) for i in range(2)])
    wb = np.concatenate(_halves(wb.reshape(512, 256)), axis=1)
    cos, sin = _trig(np.arange(32), points)
    base = np.zeros((5, 2, 8, GRID))
    base[:4, 0], base[:4, 1] = cos.reshape(4, 8, GRID), -sin.reshape(4, 8, GRID)
    cos, sin = _trig(np.array([RADIUS]), points)
    base[4, 0, 0], base[4, 1, 0] = cos[0] - 1.0, -sin[0]
    base = base.reshape(80, GRID)
    xf, xb = _left(base.T), np.concatenate(_halves(base), axis=0)
    xb = np.concatenate([xb, xb], axis=1)
    return zf, wy, xf, xb, wb, zb


def halves(value):
    high = value.astype(BF)
    return high, (value - high.astype(F32)).astype(BF)


def mm(left, right):
    return jnp.dot(left, right, preferred_element_type=F32)


OFFSETS = [(dx, dz, dc) for dc in (1, 0) for dx in (2, 1, 3, 0) for dz in (1, 0)]
CHUNKS = [o for o in OFFSETS if o[2] == 0]


def kernel(
    n_z, n_y,
    c_h, p_h, sm_h, zf_h, wy_h, xf_h, xb_h, wb_h, zb_h,
    o_ref,
    c_ref, sm_ref, zf, wy, xf, xb, wb, zb,
    xs, zs, r1, s2, r2, slab, lt, dm, m1, gs, bs, cs, sp, og,
    c_sem, a_s, a_r, b_s, b_r, gz_s, gz_r, gy_s, gy_r, own_sem,
):
    band = lax.axis_index("band")
    me = lax.axis_index("plane")
    z_me, y_me = band // n_y, lax.rem(band, n_y)
    x_at, half_at, core_at = me // 4, lax.rem(me // 2, 2), lax.rem(me, 2)
    span = c_ref.shape[0]

    def plane_peer(offset, sign=1):
        dx, dz, dc = offset
        core_to = lax.rem(core_at + dc, 2)
        sender = core_at if sign == 1 else core_to
        x_to = lax.rem(x_at + sign * dx * (1 - 2 * sender) + 4, 4)
        return x_to * 4 + lax.rem(half_at + dz + sender, 2) * 2 + core_to

    side = lax.rem(z_me, 2)
    partner = [
        lax.rem(z_me + 2, n_z) * n_y + y_me,
        (z_me + 1 - 2 * side) * n_y + y_me,
    ]
    half_of = [side, 1 - side]

    def z_peer(k):
        return lax.rem(z_me + k, n_z) * n_y + y_me

    def y_peer(k):
        return z_me * n_y + lax.rem(y_me + k, n_y)

    loads = [
        pltpu.make_async_copy(src, dst, c_sem.at[n])
        for n, (src, dst) in enumerate(
            [
                (c_h, c_ref), (sm_h, sm_ref), (zf_h, zf), (wy_h, wy),
                (xf_h, xf), (xb_h, xb), (wb_h, wb), (zb_h, zb),
            ]
        )
    ]
    for load in loads[:3]:
        load.start()

    barrier = pltpu.get_barrier_semaphore()
    for band_to in partner:
        for o in OFFSETS:
            pl.semaphore_signal(
                barrier, inc=1,
                device_id={"band": band_to, "plane": plane_peer(o)}, device_id_type=MESH,
            )
    last = lax.rem(z_me + 3 - 2 * side + n_z, n_z) * n_y + y_me
    pl.semaphore_signal(barrier, inc=1, device_id={"band": last}, device_id_type=MESH)
    for k in range(1, n_y):
        pl.semaphore_signal(barrier, inc=1, device_id={"band": y_peer(k)}, device_id_type=MESH)

    def a_copy(h, n):
        to = plane_peer(OFFSETS[n])
        return pltpu.make_async_remote_copy(
            src_ref=zs.at[half_of[h], to], dst_ref=r1.at[h, me],
            send_sem=a_s.at[h, n], recv_sem=a_r.at[h, n],
            device_id={"band": partner[h], "plane": to}, device_id_type=MESH,
        )

    def b_copy(h, n):
        to = plane_peer(OFFSETS[n])
        return pltpu.make_async_remote_copy(
            src_ref=s2.at[h, to], dst_ref=r2.at[side, me],
            send_sem=b_s.at[h, n], recv_sem=b_r.at[h, n],
            device_id={"band": partner[h], "plane": to}, device_id_type=MESH,
        )

    def gz_copy(k):
        at = lax.rem(z_me + k, 2) * 4
        return pltpu.make_async_remote_copy(
            src_ref=p_h.at[pl.ds(at, 4)], dst_ref=slab.at[y_me, z_me],
            send_sem=gz_s.at[k], recv_sem=gz_r.at[k],
            device_id={"band": z_peer(k)}, device_id_type=MESH,
        )

    def gy_copy(back, k):
        z_from = lax.rem(z_me - back + n_z, n_z)
        own = p_h.at[pl.ds(side * 4, 4)]
        return pltpu.make_async_remote_copy(
            src_ref=slab.at[y_me, z_from] if back else own, dst_ref=slab.at[y_me, z_from],
            send_sem=gy_s.at[back, k], recv_sem=gy_r.at[back, k],
            device_id={"band": y_peer(k)}, device_id_type=MESH,
        )

    own_copy = pltpu.make_async_copy(
        p_h.at[pl.ds(side * 4, 4)], slab.at[y_me, z_me], own_sem
    )

    loads[0].wait()
    loads[1].wait()
    heights = sm_ref[2:3, pl.ds(pl.multiple_of(me * 128, 128), 128)]
    live = jnp.abs(lax.broadcasted_iota(jnp.int32, (span, 128), 0) - RADIUS) <= heights
    xs[:, 64:80, :] = jnp.zeros((2, 16, 256), F32)
    for orb in range(2):
        for c in range(2):
            xs[c, 0:span, orb * 128 : orb * 128 + 128] = jnp.where(
                live, c_ref[:, 2 * orb + c, :], 0.0
            )
    high, low = halves(xs[...].reshape(160, 256))
    stacked = jnp.concatenate([high, high, low], axis=0)
    loads[2].wait()
    for h in range(2):
        zs[half_of[h]] = mm(
            zf[pl.ds(pl.multiple_of(half_of[h] * 128, 128), 128), :], stacked
        ).reshape(16, 8, 256)

    pl.semaphore_wait(barrier, 33 + n_y - 1)
    for k in range(1, n_z):
        gz_copy(k).start()
    for k in range(1, n_y):
        gy_copy(0, k).start()

    for n in range(16):
        a_copy(0, n).start()
    for load in loads[3:]:
        load.start()
    own_copy.start()

    stick_x, stick_y = sm_ref[0:1, :], sm_ref[1:2, :]
    d_of = stick_x & 7
    lane_of = ((stick_x >> 3) & 3) * 64 + stick_y + 31
    for n in range(16):
        rows = lax.broadcasted_iota(jnp.int32, (16, 2048), 0) + n * 16
        lt[n * 16 : n * 16 + 16, :] = jnp.where(rows == lane_of, 1.0, 0.0).astype(BF)
    for n in range(4):
        rows = lax.broadcasted_iota(jnp.int32, (16, 2048), 0) // 8 + n * 2
        dm[n] = jnp.where(rows == d_of, 1.0, 0.0).astype(BF)

    for back in sorted(range(1, n_z), key=lambda k: min(k, n_z - k)):
        gz_copy(back).wait_recv()
        for k in range(1, n_y):
            gy_copy(back, k).start()

    for n in range(16):
        a_copy(1, n).start()

    at_zero = lax.broadcasted_iota(jnp.int32, (64, 128), 1) == 31

    def place(h, source):
        lanes = pl.ds(pl.multiple_of(source * 128, 128), 128)
        block = r1[h, source]
        twice = jnp.concatenate([block, block], axis=0)
        for p, part in enumerate(halves(twice)):
            for orb in range(2):
                piece = part[:, orb * 128 : orb * 128 + 128]
                for n in range(4):
                    at = p * 128 + orb * 64 + n * 16
                    m1[h, at : at + 16, lanes] = piece * dm[n, :, lanes]

    def keep(h, value, at):
        high, low = halves(value)
        for orb in range(2):
            for z in range(4):
                lanes = slice(z * 256 + orb * 128, z * 256 + orb * 128 + 128)
                bs[h, at : at + 16, lanes] = high[orb, z]
                bs[h, 80 + at : 96 + at, lanes] = high[orb, z]
                bs[h, 160 + at : 176 + at, lanes] = low[orb, z]

    def to_columns(h):
        for n in reversed(range(16)):
            a_copy(h, n).wait_recv()
            place(h, plane_peer(OFFSETS[n], -1))
        both = lax.dot_general(
            m1[h], lt[...], (((1,), (1,)), ((), ())), preferred_element_type=F32
        )
        both = both[:128] + both[128:]
        for hx in range(2):
            gs[h, hx] = both[:, hx * 128 : hx * 128 + 128]
        grid = [
            jnp.concatenate(
                [
                    gs[h, hx, pl.ds(orb * 64 + c * 4 + z, 8, stride=8), :]
                    for orb in range(2)
                    for z in range(4)
                    for c in range(2)
                ],
                axis=0,
            )
            for hx in range(2)
        ]

        if h == 0:
            loads[3].wait()
        high, low = halves(jnp.concatenate(grid, axis=0))
        left = jnp.concatenate([high, high, low], axis=1)
        for i in range(2):
            turned = mm(left, wy[i]).reshape(2, 2, 4, 2, 8, 256)
            real = turned[:, :, :, 0, :, :128] - turned[:, :, :, 1, :, 128:]
            imag = turned[:, :, :, 0, :, 128:] + turned[:, :, :, 1, :, :128]
            both = jnp.concatenate([real, imag], axis=3)
            for hx in range(2):
                keep(h, both[hx], (2 * hx + i) * 16)
        keep(h, jnp.broadcast_to(grid[0][:, 31:32], (128, 128)).reshape(2, 4, 16, 128), 64)

    def through_planes(h):
        if h == 0:
            own_copy.wait()
            for back in range(n_z):
                for k in range(1, n_y):
                    gy_copy(back, k).wait_recv()
            loads[4].wait()
            loads[5].wait()

        field = mm(xf[...], bs[h])
        planes = []
        for z in range(4):
            plane = jnp.concatenate(
                [slab[b % n_y, b // n_y, z] for b in range(n_z * n_y)], axis=0
            )
            planes += [plane, plane]
        high, low = halves(field * jnp.concatenate(planes, axis=1))
        back = mm(xb[...], jnp.concatenate([high, low], axis=0))
        back = back[:80] + back[80:]
        for z in range(4):
            for orb in range(2):
                lanes = slice(z * 256 + orb * 128, z * 256 + orb * 128 + 128)
                rows = slice(orb * 32 + z * 8, orb * 32 + z * 8 + 8)
                for xl in range(4):
                    for c in range(2):
                        at = ((xl % 2) * 2 + c) * 128
                        cs[h, xl // 2, rows, at : at + 128] = back[
                            (xl * 2 + c) * 8 : (xl * 2 + c) * 8 + 8, lanes
                        ]
                for c in range(2):
                    sp[h, c, rows, :] = back[64 + c * 8 : 72 + c * 8, lanes]

        if h == 0:
            loads[6].wait()
        high, low = halves(cs[h].reshape(128, 512))
        wide = mm(jnp.concatenate([high, low], axis=0), wb[...])
        sums = wide[:128, :256] + wide[:128, 256:] + wide[128:, :256]
        for hx in range(2):
            turned = sums[hx * 64 : hx * 64 + 64]
            for c in range(2):
                part = turned[:, c * 128 : c * 128 + 128]
                if hx == 0:
                    extra = jnp.sum(sp[h, c], axis=1, keepdims=True)
                    part = part + jnp.where(at_zero, extra, 0.0)
                for orb in range(2):
                    at = orb * 64 + c * 32
                    og[h, hx, at : at + 32, :] = part[orb * 32 : orb * 32 + 32]

        picked = jnp.concatenate(
            [
                jnp.concatenate(
                    [
                        og[h, hx, pl.ds(orb * 64 + d, 8, stride=8), :]
                        for d in range(8)
                        for orb in range(2)
                    ],
                    axis=0,
                )
                for hx in range(2)
            ],
            axis=1,
        )
        picked = jnp.concatenate(halves(picked), axis=0)
        for chunk_offset in CHUNKS:
            chunk = plane_peer(chunk_offset) // 2
            lanes = pl.ds(pl.multiple_of(chunk * 256, 256), 256)
            ones = lt[:, lanes]
            wide = mm(picked, ones)
            wide = (wide[:128] + wide[128:]).reshape(8, 16, 256)
            d_here = jnp.broadcast_to(sm_ref[0:1, lanes] & 7, (16, 256))
            total = wide[0]
            for d in range(1, 8):
                total = jnp.where(d_here == d, wide[d], total)
            for core in range(2):
                for orb in range(2):
                    s2[h, chunk * 2 + core, :, orb * 128 : orb * 128 + 128] = total[
                        orb * 8 : orb * 8 + 8, core * 128 : core * 128 + 128
                    ]
            for n, o in enumerate(OFFSETS):
                if o[:2] == chunk_offset[:2]:
                    b_copy(h, n).start()

    to_columns(0)
    through_planes(0)
    to_columns(1)
    through_planes(1)

    for k in range(1, n_z):
        gz_copy(k).wait_send()
    for back in range(n_z):
        for k in range(1, n_y):
            gy_copy(back, k).wait_send()
    for h in range(2):
        for n in range(16):
            a_copy(h, n).wait_send()
    loads[7].wait()
    result = None
    for h in range(2):
        for n in range(16):
            b_copy(h, n).wait_send()
        for n in range(16):
            b_copy(h, n).wait_recv()
        high, low = halves(r2[half_of[h]].reshape(128, 256))
        part = mm(zb[half_of[h]], jnp.concatenate([high, high, low], axis=0))
        result = part if h == 0 else result + part
    result = result * (2.0 / GRID**3)
    for orb in range(2):
        for c in range(2):
            o_ref[:, 2 * orb + c, :] = jnp.where(
                live, result[c * 72 : c * 72 + span, orb * 128 : orb * 128 + 128], 0.0
            )


def per_device(n_z, n_y, coeffs, potential, stick_map):
    consts = tables()
    moved = jnp.transpose(coeffs[0], (1, 0, 2))
    vmem = pl.BlockSpec(memory_space=pltpu.VMEM)
    hbm = pl.BlockSpec(memory_space=pltpu.HBM)
    dma = pltpu.SemaphoreType.DMA
    scratch = [
        pltpu.VMEM(moved.shape, F32),
        pltpu.VMEM(stick_map.shape, jnp.int32),
    ] + [pltpu.VMEM(t.shape, BF) for t in consts] + [
        pltpu.VMEM((2, 80, 256), F32),
        pltpu.VMEM((2, 16, 8, 256), F32),
        pltpu.VMEM((2, 16, 8, 256), F32),
        pltpu.VMEM((2, 16, 8, 256), F32),
        pltpu.VMEM((2, 16, 8, 256), F32),
        pltpu.VMEM((n_y, n_z, 4) + potential.shape[1:], F32),
        pltpu.VMEM((256, 2048), BF),
        pltpu.VMEM((4, 16, 2048), BF),
        pltpu.VMEM((2, 256, 2048), BF),
        pltpu.VMEM((2, 2, 128, 128), F32),
        pltpu.VMEM((2, 240, 1024), BF),
        pltpu.VMEM((2, 2, 64, 512), F32),
        pltpu.VMEM((2, 2, 64, 128), F32),
        pltpu.VMEM((2, 2, 128, 128), F32),
        dma((len(consts) + 2,)),
        dma((2, 16)), dma((2, 16)), dma((2, 16)), dma((2, 16)),
        dma((4,)), dma((4,)), dma((4, 4)), dma((4, 4)), dma,
    ]
    result = pl.pallas_call(
        functools.partial(kernel, n_z, n_y),
        out_shape=jax.ShapeDtypeStruct(moved.shape, F32),
        in_specs=[hbm] * (len(consts) + 3),
        out_specs=vmem,
        scratch_shapes=scratch,
        compiler_params=pltpu.CompilerParams(
            collective_id=0, has_side_effects=True, vmem_limit_bytes=40 * 1024 * 1024
        ),
    )(
        *[
            pltpu.with_memory_space_constraint(value, pltpu.HBM)
            for value in (moved, potential, stick_map, *[jnp.asarray(t) for t in consts])
        ]
    )
    return jnp.transpose(result, (1, 0, 2))[None]


def solution(mesh):
    n_band = mesh.shape["band"]
    n_z = 4 if n_band == 16 else 1
    placed = (P("band", None, None, "plane"), P("plane", "band", None), P())
    return jax.shard_map(
        functools.partial(per_device, n_z, n_band // n_z),
        mesh=mesh,
        in_specs=placed,
        out_specs=P("band", None, None, "plane"),
        check_vma=False,
    )
```

```python
import functools

import jax
import jax.numpy as jnp
import ml_dtypes
import numpy as np
from jax import lax
from jax.experimental import pallas as pl
from jax.experimental.pallas import tpu as pltpu
from jax.sharding import PartitionSpec as P

MESH = pl.DeviceIdType.MESH
GRID = 128
RADIUS = 32
BF = jnp.bfloat16
F32 = jnp.float32


def _halves(table):
    high = table.astype(ml_dtypes.bfloat16)
    low = (table - high.astype(np.float64)).astype(ml_dtypes.bfloat16)
    return high, low


def _left(table):
    high, low = _halves(table)
    return np.concatenate([high, low, high], axis=1)


def _right(table):
    high, low = _halves(table)
    return np.concatenate([high, low, high], axis=0)


def _trig(left, right):
    turns = np.mod(np.outer(left, right), GRID) * (2.0 * np.pi / GRID)
    return np.cos(turns), np.sin(turns)


def tables():
    points = np.arange(GRID)
    depth = np.arange(2 * RADIUS + 1) - RADIUS
    span = depth.size
    cos, sin = _trig(points, depth)
    zf = np.zeros((16, 2, 8, 2, 80))
    cos, sin = cos.reshape(16, 8, span), sin.reshape(16, 8, span)
    zf[:, 0, :, 0, :span], zf[:, 0, :, 1, :span] = cos, -sin
    zf[:, 1, :, 0, :span], zf[:, 1, :, 1, :span] = sin, cos
    zf = zf.reshape(16, 2, 2, 4, 160).transpose(2, 0, 1, 3, 4)
    zf = _left(zf.reshape(256, 160))
    zb = np.zeros((2, 72, 16, 2, 8))
    cos, sin = np.moveaxis(cos, 2, 0), np.moveaxis(sin, 2, 0)
    zb[0, :span, :, 0], zb[0, :span, :, 1] = cos, sin
    zb[1, :span, :, 0], zb[1, :span, :, 1] = -sin, cos
    zb = zb.reshape(144, 16, 2, 2, 4).transpose(0, 3, 1, 2, 4).reshape(144, 2, 128)
    zb = np.stack([_left(zb[:, h]) for h in range(2)])
    cos, sin = _trig(np.arange(64) - 31, points)
    wy = np.zeros((2, 2, 64, 2, GRID))
    wb = np.zeros((2, 2, GRID, 2, 2, 64))
    for i in range(2):
        wy[i, i, :, 0], wy[i, i, :, 1] = cos, sin
        wb[i, 0, :, 0, i], wb[i, 1, :, 0, i] = cos.T, sin.T
        wb[i, 0, :, 1, i], wb[i, 1, :, 1, i] = -sin.T, cos.T
    wy = np.stack([_right(wy[i].reshape(128, 256)) for i in range(2)])
    wb = np.concatenate(_halves(wb.reshape(512, 256)), axis=1)
    cos, sin = _trig(np.arange(32), points)
    base = np.zeros((5, 2, 8, GRID))
    base[:4, 0], base[:4, 1] = cos.reshape(4, 8, GRID), -sin.reshape(4, 8, GRID)
    cos, sin = _trig(np.array([RADIUS]), points)
    base[4, 0, 0], base[4, 1, 0] = cos[0] - 1.0, -sin[0]
    base = base.reshape(80, GRID)
    xf, xb = _left(base.T), np.concatenate(_halves(base), axis=0)
    xb = np.concatenate([xb, xb], axis=1)
    return zf, wy, xf, xb, wb, zb


def halves(value):
    high = value.astype(BF)
    return high, (value - high.astype(F32)).astype(BF)


def mm(left, right):
    return jnp.dot(left, right, preferred_element_type=F32)


OFFSETS = [(dx, dz, dc) for dc in (1, 0) for dx in (2, 1, 3, 0) for dz in (1, 0)]
CHUNKS = [o for o in OFFSETS if o[2] == 0]


def kernel(
    n_z, n_y,
    c_h, p_h, sm_h, zf_h, wy_h, xf_h, xb_h, wb_h, zb_h,
    o_ref,
    c_ref, sm_ref, zf, wy, xf, xb, wb, zb,
    xs, zs, r1, s2, r2, slab, lt, dm, m1, gs, bs, cs, sp, og,
    c_sem, a_s, a_r, b_s, b_r, gz_s, gz_r, gy_s, gy_r, own_sem,
):
    band = lax.axis_index("band")
    me = lax.axis_index("plane")
    z_me, y_me = band // n_y, lax.rem(band, n_y)
    x_at, half_at, core_at = me // 4, lax.rem(me // 2, 2), lax.rem(me, 2)
    span = c_ref.shape[0]

    def plane_peer(offset, sign=1):
        dx, dz, dc = offset
        core_to = lax.rem(core_at + dc, 2)
        sender = core_at if sign == 1 else core_to
        x_to = lax.rem(x_at + sign * dx * (1 - 2 * sender) + 4, 4)
        return x_to * 4 + lax.rem(half_at + dz + sender, 2) * 2 + core_to

    side = lax.rem(z_me, 2)
    partner = [
        lax.rem(z_me + 2, n_z) * n_y + y_me,
        (z_me + 1 - 2 * side) * n_y + y_me,
    ]
    half_of = [side, 1 - side]

    def z_peer(k):
        return lax.rem(z_me + k, n_z) * n_y + y_me

    def y_peer(k):
        return z_me * n_y + lax.rem(y_me + k, n_y)

    loads = [
        pltpu.make_async_copy(src, dst, c_sem.at[n])
        for n, (src, dst) in enumerate(
            [
                (c_h, c_ref), (sm_h, sm_ref), (zf_h, zf), (wy_h, wy),
                (xf_h, xf), (xb_h, xb), (wb_h, wb), (zb_h, zb),
            ]
        )
    ]
    for load in loads[:3]:
        load.start()

    barrier = pltpu.get_barrier_semaphore()
    for band_to in partner:
        for o in OFFSETS:
            pl.semaphore_signal(
                barrier, inc=1,
                device_id={"band": band_to, "plane": plane_peer(o)}, device_id_type=MESH,
            )
    last = lax.rem(z_me + 3 - 2 * side + n_z, n_z) * n_y + y_me
    pl.semaphore_signal(barrier, inc=1, device_id={"band": last}, device_id_type=MESH)
    for k in range(1, n_y):
        pl.semaphore_signal(barrier, inc=1, device_id={"band": y_peer(k)}, device_id_type=MESH)

    def a_copy(h, n):
        to = plane_peer(OFFSETS[n])
        return pltpu.make_async_remote_copy(
            src_ref=zs.at[half_of[h], to], dst_ref=r1.at[h, me],
            send_sem=a_s.at[h, n], recv_sem=a_r.at[h, n],
            device_id={"band": partner[h], "plane": to}, device_id_type=MESH,
        )

    def b_copy(h, n):
        to = plane_peer(OFFSETS[n])
        return pltpu.make_async_remote_copy(
            src_ref=s2.at[h, to], dst_ref=r2.at[side, me],
            send_sem=b_s.at[h, n], recv_sem=b_r.at[h, n],
            device_id={"band": partner[h], "plane": to}, device_id_type=MESH,
        )

    def gz_copy(k):
        at = lax.rem(z_me + k, 2) * 4
        return pltpu.make_async_remote_copy(
            src_ref=p_h.at[pl.ds(at, 4)], dst_ref=slab.at[y_me, z_me],
            send_sem=gz_s.at[k], recv_sem=gz_r.at[k],
            device_id={"band": z_peer(k)}, device_id_type=MESH,
        )

    def gy_copy(back, k):
        z_from = lax.rem(z_me - back + n_z, n_z)
        own = p_h.at[pl.ds(side * 4, 4)]
        return pltpu.make_async_remote_copy(
            src_ref=slab.at[y_me, z_from] if back else own, dst_ref=slab.at[y_me, z_from],
            send_sem=gy_s.at[back, k], recv_sem=gy_r.at[back, k],
            device_id={"band": y_peer(k)}, device_id_type=MESH,
        )

    own_copy = pltpu.make_async_copy(
        p_h.at[pl.ds(side * 4, 4)], slab.at[y_me, z_me], own_sem
    )

    loads[0].wait()
    loads[1].wait()
    heights = sm_ref[2:3, pl.ds(pl.multiple_of(me * 128, 128), 128)]
    live = jnp.abs(lax.broadcasted_iota(jnp.int32, (span, 128), 0) - RADIUS) <= heights
    xs[:, 64:80, :] = jnp.zeros((2, 16, 256), F32)
    for orb in range(2):
        for c in range(2):
            xs[c, 0:span, orb * 128 : orb * 128 + 128] = jnp.where(
                live, c_ref[:, 2 * orb + c, :], 0.0
            )
    high, low = halves(xs[...].reshape(160, 256))
    stacked = jnp.concatenate([high, high, low], axis=0)
    loads[2].wait()
    for h in range(2):
        zs[half_of[h]] = mm(
            zf[pl.ds(pl.multiple_of(half_of[h] * 128, 128), 128), :], stacked
        ).reshape(16, 8, 256)

    pl.semaphore_wait(barrier, 33 + n_y - 1)
    for k in (2, 1, 3):
        gz_copy(k).start()
    for k in (2, 1, 3):
        gy_copy(0, k).start()

    for n in range(16):
        a_copy(0, n).start()
    for load in loads[3:]:
        load.start()
    own_copy.start()

    stick_x, stick_y = sm_ref[0:1, :], sm_ref[1:2, :]
    d_of = stick_x & 7
    lane_of = ((stick_x >> 3) & 3) * 64 + stick_y + 31
    for n in range(16):
        rows = lax.broadcasted_iota(jnp.int32, (16, 2048), 0) + n * 16
        lt[n * 16 : n * 16 + 16, :] = jnp.where(rows == lane_of, 1.0, 0.0).astype(BF)
    for n in range(4):
        rows = lax.broadcasted_iota(jnp.int32, (16, 2048), 0) // 8 + n * 2
        dm[n] = jnp.where(rows == d_of, 1.0, 0.0).astype(BF)

    for back in sorted(range(1, n_z), key=lambda k: min(k, n_z - k)):
        gz_copy(back).wait_recv()
        for k in (2, 1, 3):
            gy_copy(back, k).start()

    for n in range(16):
        a_copy(1, n).start()

    at_zero = lax.broadcasted_iota(jnp.int32, (64, 128), 1) == 31

    def place(h, source):
        lanes = pl.ds(pl.multiple_of(source * 128, 128), 128)
        block = r1[h, source]
        twice = jnp.concatenate([block, block], axis=0)
        for p, part in enumerate(halves(twice)):
            for orb in range(2):
                piece = part[:, orb * 128 : orb * 128 + 128]
                for n in range(4):
                    at = p * 128 + orb * 64 + n * 16
                    m1[h, at : at + 16, lanes] = piece * dm[n, :, lanes]

    def keep(h, value, at):
        high, low = halves(value)
        for orb in range(2):
            for z in range(4):
                lanes = slice(z * 256 + orb * 128, z * 256 + orb * 128 + 128)
                bs[h, at : at + 16, lanes] = high[orb, z]
                bs[h, 80 + at : 96 + at, lanes] = high[orb, z]
                bs[h, 160 + at : 176 + at, lanes] = low[orb, z]

    def to_columns(h):
        for n in reversed(range(16)):
            a_copy(h, n).wait_recv()
            place(h, plane_peer(OFFSETS[n], -1))
        both = lax.dot_general(
            m1[h], lt[...], (((1,), (1,)), ((), ())), preferred_element_type=F32
        )
        both = both[:128] + both[128:]
        for hx in range(2):
            gs[h, hx] = both[:, hx * 128 : hx * 128 + 128]
        grid = [
            jnp.concatenate(
                [
                    gs[h, hx, pl.ds(orb * 64 + c * 4 + z, 8, stride=8), :]
                    for orb in range(2)
                    for z in range(4)
                    for c in range(2)
                ],
                axis=0,
            )
            for hx in range(2)
        ]

        if h == 0:
            loads[3].wait()
        high, low = halves(jnp.concatenate(grid, axis=0))
        left = jnp.concatenate([high, high, low], axis=1)
        for i in range(2):
            turned = mm(left, wy[i]).reshape(2, 2, 4, 2, 8, 256)
            real = turned[:, :, :, 0, :, :128] - turned[:, :, :, 1, :, 128:]
            imag = turned[:, :, :, 0, :, 128:] + turned[:, :, :, 1, :, :128]
            both = jnp.concatenate([real, imag], axis=3)
            for hx in range(2):
                keep(h, both[hx], (2 * hx + i) * 16)
        keep(h, jnp.broadcast_to(grid[0][:, 31:32], (128, 128)).reshape(2, 4, 16, 128), 64)

    def through_planes(h):
        if h == 0:
            own_copy.wait()
            for back in range(n_z):
                for k in range(1, n_y):
                    gy_copy(back, k).wait_recv()
            loads[4].wait()
            loads[5].wait()

        field = mm(xf[...], bs[h])
        planes = []
        for z in range(4):
            plane = jnp.concatenate(
                [slab[b % n_y, b // n_y, z] for b in range(n_z * n_y)], axis=0
            )
            planes += [plane, plane]
        high, low = halves(field * jnp.concatenate(planes, axis=1))
        back = mm(xb[...], jnp.concatenate([high, low], axis=0))
        back = back[:80] + back[80:]
        for z in range(4):
            for orb in range(2):
                lanes = slice(z * 256 + orb * 128, z * 256 + orb * 128 + 128)
                rows = slice(orb * 32 + z * 8, orb * 32 + z * 8 + 8)
                for xl in range(4):
                    for c in range(2):
                        at = ((xl % 2) * 2 + c) * 128
                        cs[h, xl // 2, rows, at : at + 128] = back[
                            (xl * 2 + c) * 8 : (xl * 2 + c) * 8 + 8, lanes
                        ]
                for c in range(2):
                    sp[h, c, rows, :] = back[64 + c * 8 : 72 + c * 8, lanes]

        if h == 0:
            loads[6].wait()
        high, low = halves(cs[h].reshape(128, 512))
        wide = mm(jnp.concatenate([high, low], axis=0), wb[...])
        sums = wide[:128, :256] + wide[:128, 256:] + wide[128:, :256]
        for hx in range(2):
            turned = sums[hx * 64 : hx * 64 + 64]
            for c in range(2):
                part = turned[:, c * 128 : c * 128 + 128]
                if hx == 0:
                    extra = jnp.sum(sp[h, c], axis=1, keepdims=True)
                    part = part + jnp.where(at_zero, extra, 0.0)
                for orb in range(2):
                    at = orb * 64 + c * 32
                    og[h, hx, at : at + 32, :] = part[orb * 32 : orb * 32 + 32]

        picked = jnp.concatenate(
            [
                jnp.concatenate(
                    [
                        og[h, hx, pl.ds(orb * 64 + d, 8, stride=8), :]
                        for d in range(8)
                        for orb in range(2)
                    ],
                    axis=0,
                )
                for hx in range(2)
            ],
            axis=1,
        )
        picked = jnp.concatenate(halves(picked), axis=0)
        for chunk_offset in CHUNKS:
            chunk = plane_peer(chunk_offset) // 2
            lanes = pl.ds(pl.multiple_of(chunk * 256, 256), 256)
            ones = lt[:, lanes]
            wide = mm(picked, ones)
            wide = (wide[:128] + wide[128:]).reshape(8, 16, 256)
            d_here = jnp.broadcast_to(sm_ref[0:1, lanes] & 7, (16, 256))
            total = wide[0]
            for d in range(1, 8):
                total = jnp.where(d_here == d, wide[d], total)
            for core in range(2):
                for orb in range(2):
                    s2[h, chunk * 2 + core, :, orb * 128 : orb * 128 + 128] = total[
                        orb * 8 : orb * 8 + 8, core * 128 : core * 128 + 128
                    ]
            for n, o in enumerate(OFFSETS):
                if o[:2] == chunk_offset[:2]:
                    b_copy(h, n).start()

    to_columns(0)
    through_planes(0)
    to_columns(1)
    through_planes(1)

    for k in range(1, n_z):
        gz_copy(k).wait_send()
    for back in range(n_z):
        for k in range(1, n_y):
            gy_copy(back, k).wait_send()
    for h in range(2):
        for n in range(16):
            a_copy(h, n).wait_send()
    loads[7].wait()
    result = None
    for h in range(2):
        for n in range(16):
            b_copy(h, n).wait_send()
        for n in range(16):
            b_copy(h, n).wait_recv()
        high, low = halves(r2[half_of[h]].reshape(128, 256))
        part = mm(zb[half_of[h]], jnp.concatenate([high, high, low], axis=0))
        result = part if h == 0 else result + part
    result = result * (2.0 / GRID**3)
    for orb in range(2):
        for c in range(2):
            o_ref[:, 2 * orb + c, :] = jnp.where(
                live, result[c * 72 : c * 72 + span, orb * 128 : orb * 128 + 128], 0.0
            )


def per_device(n_z, n_y, coeffs, potential, stick_map):
    consts = tables()
    moved = jnp.transpose(coeffs[0], (1, 0, 2))
    vmem = pl.BlockSpec(memory_space=pltpu.VMEM)
    hbm = pl.BlockSpec(memory_space=pltpu.HBM)
    dma = pltpu.SemaphoreType.DMA
    scratch = [
        pltpu.VMEM(moved.shape, F32),
        pltpu.VMEM(stick_map.shape, jnp.int32),
    ] + [pltpu.VMEM(t.shape, BF) for t in consts] + [
        pltpu.VMEM((2, 80, 256), F32),
        pltpu.VMEM((2, 16, 8, 256), F32),
        pltpu.VMEM((2, 16, 8, 256), F32),
        pltpu.VMEM((2, 16, 8, 256), F32),
        pltpu.VMEM((2, 16, 8, 256), F32),
        pltpu.VMEM((n_y, n_z, 4) + potential.shape[1:], F32),
        pltpu.VMEM((256, 2048), BF),
        pltpu.VMEM((4, 16, 2048), BF),
        pltpu.VMEM((2, 256, 2048), BF),
        pltpu.VMEM((2, 2, 128, 128), F32),
        pltpu.VMEM((2, 240, 1024), BF),
        pltpu.VMEM((2, 2, 64, 512), F32),
        pltpu.VMEM((2, 2, 64, 128), F32),
        pltpu.VMEM((2, 2, 128, 128), F32),
        dma((len(consts) + 2,)),
        dma((2, 16)), dma((2, 16)), dma((2, 16)), dma((2, 16)),
        dma((4,)), dma((4,)), dma((4, 4)), dma((4, 4)), dma,
    ]
    result = pl.pallas_call(
        functools.partial(kernel, n_z, n_y),
        out_shape=jax.ShapeDtypeStruct(moved.shape, F32),
        in_specs=[hbm] * (len(consts) + 3),
        out_specs=vmem,
        scratch_shapes=scratch,
        compiler_params=pltpu.CompilerParams(
            collective_id=0, has_side_effects=True, vmem_limit_bytes=40 * 1024 * 1024
        ),
    )(
        *[
            pltpu.with_memory_space_constraint(value, pltpu.HBM)
            for value in (moved, potential, stick_map, *[jnp.asarray(t) for t in consts])
        ]
    )
    return jnp.transpose(result, (1, 0, 2))[None]


def solution(mesh):
    n_band = mesh.shape["band"]
    n_z = 4 if n_band == 16 else 1
    placed = (P("band", None, None, "plane"), P("plane", "band", None), P())
    return jax.shard_map(
        functools.partial(per_device, n_z, n_band // n_z),
        mesh=mesh,
        in_specs=placed,
        out_specs=P("band", None, None, "plane"),
        check_vma=False,
    )
```

```python
import functools

import jax
import jax.numpy as jnp
import ml_dtypes
import numpy as np
from jax import lax
from jax.experimental import pallas as pl
from jax.experimental.pallas import tpu as pltpu
from jax.sharding import PartitionSpec as P

MESH = pl.DeviceIdType.MESH
GRID = 128
RADIUS = 32
BF = jnp.bfloat16
F32 = jnp.float32


def _halves(table):
    high = table.astype(ml_dtypes.bfloat16)
    low = (table - high.astype(np.float64)).astype(ml_dtypes.bfloat16)
    return high, low


def _left(table):
    high, low = _halves(table)
    return np.concatenate([high, low, high], axis=1)


def _right(table):
    high, low = _halves(table)
    return np.concatenate([high, low, high], axis=0)


def _trig(left, right):
    turns = np.mod(np.outer(left, right), GRID) * (2.0 * np.pi / GRID)
    return np.cos(turns), np.sin(turns)


def tables():
    points = np.arange(GRID)
    depth = np.arange(2 * RADIUS + 1) - RADIUS
    span = depth.size
    cos, sin = _trig(points, depth)
    zf = np.zeros((16, 2, 8, 2, 80))
    cos, sin = cos.reshape(16, 8, span), sin.reshape(16, 8, span)
    zf[:, 0, :, 0, :span], zf[:, 0, :, 1, :span] = cos, -sin
    zf[:, 1, :, 0, :span], zf[:, 1, :, 1, :span] = sin, cos
    zf = zf.reshape(16, 2, 2, 4, 160).transpose(2, 0, 1, 3, 4)
    zf = _left(zf.reshape(256, 160))
    zb = np.zeros((2, 72, 16, 2, 8))
    cos, sin = np.moveaxis(cos, 2, 0), np.moveaxis(sin, 2, 0)
    zb[0, :span, :, 0], zb[0, :span, :, 1] = cos, sin
    zb[1, :span, :, 0], zb[1, :span, :, 1] = -sin, cos
    zb = zb.reshape(144, 16, 2, 2, 4).transpose(0, 3, 1, 2, 4).reshape(144, 2, 128)
    zb = np.stack([_left(zb[:, h]) for h in range(2)])
    cos, sin = _trig(np.arange(64) - 31, points)
    wy = np.zeros((2, 2, 64, 2, GRID))
    wb = np.zeros((2, 2, GRID, 2, 2, 64))
    for i in range(2):
        wy[i, i, :, 0], wy[i, i, :, 1] = cos, sin
        wb[i, 0, :, 0, i], wb[i, 1, :, 0, i] = cos.T, sin.T
        wb[i, 0, :, 1, i], wb[i, 1, :, 1, i] = -sin.T, cos.T
    wy = np.stack([_right(wy[i].reshape(128, 256)) for i in range(2)])
    wb = np.concatenate(_halves(wb.reshape(512, 256)), axis=1)
    cos, sin = _trig(np.arange(32), points)
    base = np.zeros((5, 2, 8, GRID))
    base[:4, 0], base[:4, 1] = cos.reshape(4, 8, GRID), -sin.reshape(4, 8, GRID)
    cos, sin = _trig(np.array([RADIUS]), points)
    base[4, 0, 0], base[4, 1, 0] = cos[0] - 1.0, -sin[0]
    base = base.reshape(80, GRID)
    xf, xb = _left(base.T), np.concatenate(_halves(base), axis=0)
    xb = np.concatenate([xb, xb], axis=1)
    return zf, wy, xf, xb, wb, zb


def halves(value):
    high = value.astype(BF)
    return high, (value - high.astype(F32)).astype(BF)


def mm(left, right):
    return jnp.dot(left, right, preferred_element_type=F32)


OFFSETS = [(dx, dz, dc) for dx in (2, 1, 3, 0) for dz in (1, 0) for dc in (1, 0)]
CHUNKS = [o for o in OFFSETS if o[2] == 0]


def kernel(
    n_z, n_y,
    c_h, p_h, sm_h, zf_h, wy_h, xf_h, xb_h, wb_h, zb_h,
    o_ref,
    c_ref, sm_ref, zf, wy, xf, xb, wb, zb,
    xs, zs, r1, s2, r2, slab, lt, dm, m1, gs, bs, cs, sp, og,
    c_sem, a_s, a_r, b_s, b_r, gz_s, gz_r, gy_s, gy_r, own_sem,
):
    band = lax.axis_index("band")
    me = lax.axis_index("plane")
    z_me, y_me = band // n_y, lax.rem(band, n_y)
    x_at, half_at, core_at = me // 4, lax.rem(me // 2, 2), lax.rem(me, 2)
    span = c_ref.shape[0]

    def plane_peer(offset, sign=1):
        dx, dz, dc = offset
        core_to = lax.rem(core_at + dc, 2)
        sender = core_at if sign == 1 else core_to
        x_to = lax.rem(x_at + sign * dx * (1 - 2 * sender) + 4, 4)
        return x_to * 4 + lax.rem(half_at + dz + sender, 2) * 2 + core_to

    side = lax.rem(z_me, 2)
    partner = [
        lax.rem(z_me + 2, n_z) * n_y + y_me,
        (z_me + 1 - 2 * side) * n_y + y_me,
    ]
    half_of = [side, 1 - side]

    def z_peer(k):
        return lax.rem(z_me + k, n_z) * n_y + y_me

    def y_peer(k):
        return z_me * n_y + lax.rem(y_me + k, n_y)

    loads = [
        pltpu.make_async_copy(src, dst, c_sem.at[n])
        for n, (src, dst) in enumerate(
            [
                (c_h, c_ref), (sm_h, sm_ref), (zf_h, zf), (wy_h, wy),
                (xf_h, xf), (xb_h, xb), (wb_h, wb), (zb_h, zb),
            ]
        )
    ]
    for load in loads[:3]:
        load.start()

    barrier = pltpu.get_barrier_semaphore()
    for band_to in partner:
        for o in OFFSETS:
            pl.semaphore_signal(
                barrier, inc=1,
                device_id={"band": band_to, "plane": plane_peer(o)}, device_id_type=MESH,
            )
    last = lax.rem(z_me + 3 - 2 * side + n_z, n_z) * n_y + y_me
    pl.semaphore_signal(barrier, inc=1, device_id={"band": last}, device_id_type=MESH)
    for k in range(1, n_y):
        pl.semaphore_signal(barrier, inc=1, device_id={"band": y_peer(k)}, device_id_type=MESH)

    def a_copy(h, n):
        to = plane_peer(OFFSETS[n])
        return pltpu.make_async_remote_copy(
            src_ref=zs.at[half_of[h], to], dst_ref=r1.at[h, me],
            send_sem=a_s.at[h, n], recv_sem=a_r.at[h, n],
            device_id={"band": partner[h], "plane": to}, device_id_type=MESH,
        )

    def b_copy(h, n):
        to = plane_peer(OFFSETS[n])
        return pltpu.make_async_remote_copy(
            src_ref=s2.at[h, to], dst_ref=r2.at[side, me],
            send_sem=b_s.at[h, n], recv_sem=b_r.at[h, n],
            device_id={"band": partner[h], "plane": to}, device_id_type=MESH,
        )

    def gz_copy(k):
        at = lax.rem(z_me + k, 2) * 4
        return pltpu.make_async_remote_copy(
            src_ref=p_h.at[pl.ds(at, 4)], dst_ref=slab.at[y_me, z_me],
            send_sem=gz_s.at[k], recv_sem=gz_r.at[k],
            device_id={"band": z_peer(k)}, device_id_type=MESH,
        )

    def gy_copy(back, k):
        z_from = lax.rem(z_me - back + n_z, n_z)
        own = p_h.at[pl.ds(side * 4, 4)]
        return pltpu.make_async_remote_copy(
            src_ref=slab.at[y_me, z_from] if back else own, dst_ref=slab.at[y_me, z_from],
            send_sem=gy_s.at[back, k], recv_sem=gy_r.at[back, k],
            device_id={"band": y_peer(k)}, device_id_type=MESH,
        )

    own_copy = pltpu.make_async_copy(
        p_h.at[pl.ds(side * 4, 4)], slab.at[y_me, z_me], own_sem
    )

    loads[0].wait()
    loads[1].wait()
    heights = sm_ref[2:3, pl.ds(pl.multiple_of(me * 128, 128), 128)]
    live = jnp.abs(lax.broadcasted_iota(jnp.int32, (span, 128), 0) - RADIUS) <= heights
    xs[:, 64:80, :] = jnp.zeros((2, 16, 256), F32)
    for orb in range(2):
        for c in range(2):
            xs[c, 0:span, orb * 128 : orb * 128 + 128] = jnp.where(
                live, c_ref[:, 2 * orb + c, :], 0.0
            )
    high, low = halves(xs[...].reshape(160, 256))
    stacked = jnp.concatenate([high, high, low], axis=0)
    loads[2].wait()
    for h in range(2):
        zs[half_of[h]] = mm(
            zf[pl.ds(pl.multiple_of(half_of[h] * 128, 128), 128), :], stacked
        ).reshape(16, 8, 256)

    pl.semaphore_wait(barrier, 33 + n_y - 1)
    for k in (2, 1, 3):
        gz_copy(k).start()
    for k in (2, 1, 3):
        gy_copy(0, k).start()

    for n in range(16):
        a_copy(0, n).start()
    for load in loads[3:]:
        load.start()
    own_copy.start()

    stick_x, stick_y = sm_ref[0:1, :], sm_ref[1:2, :]
    d_of = stick_x & 7
    lane_of = ((stick_x >> 3) & 3) * 64 + stick_y + 31
    for n in range(16):
        rows = lax.broadcasted_iota(jnp.int32, (16, 2048), 0) + n * 16
        lt[n * 16 : n * 16 + 16, :] = jnp.where(rows == lane_of, 1.0, 0.0).astype(BF)
    for n in range(4):
        rows = lax.broadcasted_iota(jnp.int32, (16, 2048), 0) // 8 + n * 2
        dm[n] = jnp.where(rows == d_of, 1.0, 0.0).astype(BF)

    for back in sorted(range(1, n_z), key=lambda k: min(k, n_z - k)):
        gz_copy(back).wait_recv()
        for k in (2, 1, 3):
            gy_copy(back, k).start()

    for n in range(16):
        a_copy(1, n).start()

    at_zero = lax.broadcasted_iota(jnp.int32, (64, 128), 1) == 31

    def place(h, source):
        lanes = pl.ds(pl.multiple_of(source * 128, 128), 128)
        block = r1[h, source]
        twice = jnp.concatenate([block, block], axis=0)
        for p, part in enumerate(halves(twice)):
            for orb in range(2):
                piece = part[:, orb * 128 : orb * 128 + 128]
                for n in range(4):
                    at = p * 128 + orb * 64 + n * 16
                    m1[h, at : at + 16, lanes] = piece * dm[n, :, lanes]

    def keep(h, value, at):
        high, low = halves(value)
        for orb in range(2):
            for z in range(4):
                lanes = slice(z * 256 + orb * 128, z * 256 + orb * 128 + 128)
                bs[h, at : at + 16, lanes] = high[orb, z]
                bs[h, 80 + at : 96 + at, lanes] = high[orb, z]
                bs[h, 160 + at : 176 + at, lanes] = low[orb, z]

    def to_columns(h):
        for n in reversed(range(16)):
            a_copy(h, n).wait_recv()
            place(h, plane_peer(OFFSETS[n], -1))
        both = lax.dot_general(
            m1[h], lt[...], (((1,), (1,)), ((), ())), preferred_element_type=F32
        )
        both = both[:128] + both[128:]
        for hx in range(2):
            gs[h, hx] = both[:, hx * 128 : hx * 128 + 128]
        grid = [
            jnp.concatenate(
                [
                    gs[h, hx, pl.ds(orb * 64 + c * 4 + z, 8, stride=8), :]
                    for orb in range(2)
                    for z in range(4)
                    for c in range(2)
                ],
                axis=0,
            )
            for hx in range(2)
        ]

        if h == 0:
            loads[3].wait()
        high, low = halves(jnp.concatenate(grid, axis=0))
        left = jnp.concatenate([high, high, low], axis=1)
        for i in range(2):
            turned = mm(left, wy[i]).reshape(2, 2, 4, 2, 8, 256)
            real = turned[:, :, :, 0, :, :128] - turned[:, :, :, 1, :, 128:]
            imag = turned[:, :, :, 0, :, 128:] + turned[:, :, :, 1, :, :128]
            both = jnp.concatenate([real, imag], axis=3)
            for hx in range(2):
                keep(h, both[hx], (2 * hx + i) * 16)
        keep(h, jnp.broadcast_to(grid[0][:, 31:32], (128, 128)).reshape(2, 4, 16, 128), 64)

    def through_planes(h):
        if h == 0:
            own_copy.wait()
            for back in range(n_z):
                for k in range(1, n_y):
                    gy_copy(back, k).wait_recv()
            loads[4].wait()
            loads[5].wait()

        field = mm(xf[...], bs[h])
        planes = []
        for z in range(4):
            plane = jnp.concatenate(
                [slab[b % n_y, b // n_y, z] for b in range(n_z * n_y)], axis=0
            )
            planes += [plane, plane]
        high, low = halves(field * jnp.concatenate(planes, axis=1))
        back = mm(xb[...], jnp.concatenate([high, low], axis=0))
        back = back[:80] + back[80:]
        for z in range(4):
            for orb in range(2):
                lanes = slice(z * 256 + orb * 128, z * 256 + orb * 128 + 128)
                rows = slice(orb * 32 + z * 8, orb * 32 + z * 8 + 8)
                for xl in range(4):
                    for c in range(2):
                        at = ((xl % 2) * 2 + c) * 128
                        cs[h, xl // 2, rows, at : at + 128] = back[
                            (xl * 2 + c) * 8 : (xl * 2 + c) * 8 + 8, lanes
                        ]
                for c in range(2):
                    sp[h, c, rows, :] = back[64 + c * 8 : 72 + c * 8, lanes]

        if h == 0:
            loads[6].wait()
        high, low = halves(cs[h].reshape(128, 512))
        wide = mm(jnp.concatenate([high, low], axis=0), wb[...])
        sums = wide[:128, :256] + wide[:128, 256:] + wide[128:, :256]
        for hx in range(2):
            turned = sums[hx * 64 : hx * 64 + 64]
            for c in range(2):
                part = turned[:, c * 128 : c * 128 + 128]
                if hx == 0:
                    extra = jnp.sum(sp[h, c], axis=1, keepdims=True)
                    part = part + jnp.where(at_zero, extra, 0.0)
                for orb in range(2):
                    at = orb * 64 + c * 32
                    og[h, hx, at : at + 32, :] = part[orb * 32 : orb * 32 + 32]

        picked = jnp.concatenate(
            [
                jnp.concatenate(
                    [
                        og[h, hx, pl.ds(orb * 64 + d, 8, stride=8), :]
                        for d in range(8)
                        for orb in range(2)
                    ],
                    axis=0,
                )
                for hx in range(2)
            ],
            axis=1,
        )
        picked = jnp.concatenate(halves(picked), axis=0)
        for chunk_offset in CHUNKS:
            chunk = plane_peer(chunk_offset) // 2
            lanes = pl.ds(pl.multiple_of(chunk * 256, 256), 256)
            ones = lt[:, lanes]
            wide = mm(picked, ones)
            wide = (wide[:128] + wide[128:]).reshape(8, 16, 256)
            d_here = jnp.broadcast_to(sm_ref[0:1, lanes] & 7, (16, 256))
            total = wide[0]
            for d in range(1, 8):
                total = jnp.where(d_here == d, wide[d], total)
            for core in range(2):
                for orb in range(2):
                    s2[h, chunk * 2 + core, :, orb * 128 : orb * 128 + 128] = total[
                        orb * 8 : orb * 8 + 8, core * 128 : core * 128 + 128
                    ]
            for n, o in enumerate(OFFSETS):
                if o[:2] == chunk_offset[:2]:
                    b_copy(h, n).start()

    to_columns(0)
    through_planes(0)
    to_columns(1)
    through_planes(1)

    for k in range(1, n_z):
        gz_copy(k).wait_send()
    for back in range(n_z):
        for k in range(1, n_y):
            gy_copy(back, k).wait_send()
    for h in range(2):
        for n in range(16):
            a_copy(h, n).wait_send()
    loads[7].wait()
    result = None
    for h in range(2):
        for n in range(16):
            b_copy(h, n).wait_send()
        for n in range(16):
            b_copy(h, n).wait_recv()
        high, low = halves(r2[half_of[h]].reshape(128, 256))
        part = mm(zb[half_of[h]], jnp.concatenate([high, high, low], axis=0))
        result = part if h == 0 else result + part
    result = result * (2.0 / GRID**3)
    for orb in range(2):
        for c in range(2):
            o_ref[:, 2 * orb + c, :] = jnp.where(
                live, result[c * 72 : c * 72 + span, orb * 128 : orb * 128 + 128], 0.0
            )


def per_device(n_z, n_y, coeffs, potential, stick_map):
    consts = tables()
    moved = jnp.transpose(coeffs[0], (1, 0, 2))
    vmem = pl.BlockSpec(memory_space=pltpu.VMEM)
    hbm = pl.BlockSpec(memory_space=pltpu.HBM)
    dma = pltpu.SemaphoreType.DMA
    scratch = [
        pltpu.VMEM(moved.shape, F32),
        pltpu.VMEM(stick_map.shape, jnp.int32),
    ] + [pltpu.VMEM(t.shape, BF) for t in consts] + [
        pltpu.VMEM((2, 80, 256), F32),
        pltpu.VMEM((2, 16, 8, 256), F32),
        pltpu.VMEM((2, 16, 8, 256), F32),
        pltpu.VMEM((2, 16, 8, 256), F32),
        pltpu.VMEM((2, 16, 8, 256), F32),
        pltpu.VMEM((n_y, n_z, 4) + potential.shape[1:], F32),
        pltpu.VMEM((256, 2048), BF),
        pltpu.VMEM((4, 16, 2048), BF),
        pltpu.VMEM((2, 256, 2048), BF),
        pltpu.VMEM((2, 2, 128, 128), F32),
        pltpu.VMEM((2, 240, 1024), BF),
        pltpu.VMEM((2, 2, 64, 512), F32),
        pltpu.VMEM((2, 2, 64, 128), F32),
        pltpu.VMEM((2, 2, 128, 128), F32),
        dma((len(consts) + 2,)),
        dma((2, 16)), dma((2, 16)), dma((2, 16)), dma((2, 16)),
        dma((4,)), dma((4,)), dma((4, 4)), dma((4, 4)), dma,
    ]
    result = pl.pallas_call(
        functools.partial(kernel, n_z, n_y),
        out_shape=jax.ShapeDtypeStruct(moved.shape, F32),
        in_specs=[hbm] * (len(consts) + 3),
        out_specs=vmem,
        scratch_shapes=scratch,
        compiler_params=pltpu.CompilerParams(
            collective_id=0, has_side_effects=True, vmem_limit_bytes=40 * 1024 * 1024
        ),
    )(
        *[
            pltpu.with_memory_space_constraint(value, pltpu.HBM)
            for value in (moved, potential, stick_map, *[jnp.asarray(t) for t in consts])
        ]
    )
    return jnp.transpose(result, (1, 0, 2))[None]


def solution(mesh):
    n_band = mesh.shape["band"]
    n_z = 4 if n_band == 16 else 1
    placed = (P("band", None, None, "plane"), P("plane", "band", None), P())
    return jax.shard_map(
        functools.partial(per_device, n_z, n_band // n_z),
        mesh=mesh,
        in_specs=placed,
        out_specs=P("band", None, None, "plane"),
        check_vma=False,
    )
```
